32 devices in a mesh: dom: 2 (over y), energy: 16 (over z, x, core).
Axes of the slice: x: 2, y: 2, z: 4, core: 2. Of those that a mesh axis runs over, the one named last changes fastest.
Arguments:
- hamiltonian: float32 [2, 128, 128], P('dom'), may hold values from -0.5 to 0.5
- coupling: float32 [2, 64, 64], P('dom'), may hold values from -0.75 to 0.75
- contact_rates: float32 [2, 64], replicated, may hold values from 0.2 to 2
- occupation: float32 [1, 16, 2], P(None, 'energy'), may hold values from 0 to 1
- lesser_in: float32 [1, 16, 2, 2, 128, 128], P(None, 'energy', 'dom'), may hold values from -1 to 1, as said below
- greater_in: float32 [1, 16, 2, 2, 128, 128], P(None, 'energy', 'dom'), may hold values from -1 to 1, as said below
- phonon_shift: int32 [1], replicated, may hold values from 1 to 7
Outputs:
- lesser_out: float32 [1, 16, 2, 2, 128, 128], P(None, 'energy', 'dom')
- greater_out: float32 [1, 16, 2, 2, 128, 128], P(None, 'energy', 'dom')
The draws below stay inside these ranges and needn't reach their ends.
Inputs may be any that keep to these rules, and one draw needn't show every extreme that they name: Each block of lesser_in is i times a Hermitian positive semidefinite matrix. Each block of greater_in is -i times a Hermitian positive semidefinite matrix. phonon_shift is below 8.
All inputs are finite; a program needn't handle non-finite values.
Results may differ from the reference program's by a relative error of at most 0.00027.
Values sent between devices are 32-bit elements; how exact they have to be, the bound alone decides.
A program may use at most 64 MiB of HBM per device.

```python
import math
import jax
import jax.numpy as jnp
from jax import lax

M = 128
INTERFACE = 64
E_DEV = 1
NB = 2
KMAX = 8
N_ENERGY = 16


def hermitian_blocks(key, sign_factor):
    block_count = E_DEV * N_ENERGY * NB
    key_level, key_real, key_imag = jax.random.split(key, 3)
    levels = jnp.exp(jax.random.uniform(key_level, (block_count, M), jnp.float32, 0.0, math.log(3.0)))
    spread = 0.05 / math.sqrt(M)
    raw_real = spread * jax.random.normal(key_real, (block_count, M, M), jnp.float32)
    raw_imag = spread * jax.random.normal(key_imag, (block_count, M, M), jnp.float32)
    sym_real = 0.5 * (raw_real + jnp.swapaxes(raw_real, 1, 2))
    skew_imag = 0.5 * (raw_imag - jnp.swapaxes(raw_imag, 1, 2))
    diagonal = 0.13 * levels[:, :, None] * jnp.eye(M, dtype=jnp.float32)
    positive_real = diagonal + sym_real
    positive_imag = skew_imag
    stacked = jnp.stack([-sign_factor * positive_imag, sign_factor * positive_real], 1)
    return stacked.reshape(E_DEV, N_ENERGY, NB, 2, M, M)


def draw_lesser_in(key, part):
    return hermitian_blocks(jax.random.fold_in(key, 11), 1.0)


def draw_greater_in(key, part):
    return hermitian_blocks(jax.random.fold_in(key, 23), -1.0)


def block_levels(stream_key, shape, cuts, least, largest):
    level, own = 1.0, jax.random.fold_in(stream_key, 6)
    for axis_at, parts in cuts:
        heights = jnp.exp(jax.random.uniform(jax.random.fold_in(own, axis_at), (parts,), jnp.float32, least / len(cuts), largest / len(cuts)))
        level = level * jnp.repeat(heights, shape[axis_at] // parts).reshape([-1 if axis == axis_at else 1 for axis in range(len(shape))])
    return level


def gaussian(rng, extent, scale, reach, cuts=(), kind=jnp.bfloat16):
    entries = jax.random.normal(rng, extent, jnp.float32) * scale
    if len(cuts) > 0:
        entries = block_levels(rng, extent, cuts, -0.22, 0.18) * entries
    return jnp.clip(entries, min=-reach, max=reach).astype(kind)


def setup_inputs(seed: int = 0) -> dict:
    key_list = jax.random.split(jax.random.key(seed), 8)
    return {
        "hamiltonian": gaussian(key_list[0], (NB, M, M), M ** -0.5, 0.5, ((0, 2),), jnp.float32),
        "coupling": gaussian(key_list[1], (NB, INTERFACE, INTERFACE), INTERFACE ** -0.5, 0.75, ((0, 2),), jnp.float32),
        "contact_rates": jnp.clip(jnp.exp(jax.random.uniform(key_list[2], (2, INTERFACE), jnp.float32, math.log(0.2), math.log(2.0))), 0.2, 2.0),
        "occupation": jnp.clip(1.0 * jax.random.uniform(key_list[3], (E_DEV, N_ENERGY, 2), jnp.float32) ** block_levels(key_list[3], (E_DEV, N_ENERGY, 2), ((1, 16),), -0.2, 0.2), 0.0, 1.0),
        "lesser_in": draw_lesser_in(jax.random.fold_in(key_list[7], 71), 0),
        "greater_in": draw_greater_in(jax.random.fold_in(key_list[7], 71), 0),
        "phonon_shift": jax.random.randint(key_list[6], (1,), 1, KMAX).astype(jnp.int32),
    }


highest = lax.Precision.HIGHEST
broadening = 0.2
phonon_bose = 0.4
phonon_strength = 0.5

def matmul_high(first_factor, second_factor):
    return jnp.matmul(first_factor, second_factor, precision=highest)

def transposed(matrix):
    return jnp.swapaxes(matrix, -1, -2)

def complex_product(first_pair, second_pair):
    return (matmul_high(first_pair[0], second_pair[0]) - matmul_high(first_pair[1], second_pair[1]), matmul_high(first_pair[0], second_pair[1]) + matmul_high(first_pair[1], second_pair[0]))

def adjoint(complex_pair):
    return (transposed(complex_pair[0]), -transposed(complex_pair[1]))

def inverted(complex_pair):
    real_part, imag_part = complex_pair
    orbitals = real_part.shape[-1]
    stacked = jnp.concatenate([jnp.concatenate([real_part, -imag_part], -1), jnp.concatenate([imag_part, real_part], -1)], -2)
    target = jnp.concatenate([jnp.eye(orbitals, dtype=jnp.float32), jnp.zeros((orbitals, orbitals), jnp.float32)], 0)
    target = jnp.broadcast_to(target, stacked.shape[:-2] + target.shape)
    solved = jnp.linalg.solve(stacked, target)
    return (solved[..., :orbitals, :], solved[..., orbitals:, :])

def pad_first(corner, orbitals):
    extra = orbitals - corner.shape[-1]
    return jnp.pad(corner, ((0, 0), (0, extra), (0, extra)))

def pad_last(corner, orbitals):
    extra = orbitals - corner.shape[-1]
    return jnp.pad(corner, ((0, 0), (extra, 0), (extra, 0)))

def reference(hamiltonian, coupling, contact_rates, occupation, lesser_in, greater_in, phonon_shift):
    blocks = hamiltonian.shape[0]
    orbitals = hamiltonian.shape[1]
    interface = coupling.shape[1]
    energies = lesser_in.shape[0] * lesser_in.shape[1]
    lesser_all = jnp.swapaxes(lesser_in.reshape((energies,) + lesser_in.shape[2:]), 0, 1)
    greater_all = jnp.swapaxes(greater_in.reshape((energies,) + greater_in.shape[2:]), 0, 1)
    filling = occupation.reshape(energies, 2)
    energy_index = jnp.arange(energies, dtype=jnp.int32)
    energy_value = -1.5 + 3.0 * energy_index.astype(jnp.float32) / (energies - 1)
    identity = jnp.eye(orbitals, dtype=jnp.float32)
    extra = orbitals - interface
    gamma_left = jnp.pad(jnp.diag(contact_rates[0]), ((0, extra), (0, extra)))
    last_coupling = coupling[blocks - 1]
    gamma_right = jnp.pad(matmul_high(last_coupling * contact_rates[1][None, :], transposed(last_coupling)), ((extra, 0), (extra, 0)))
    block_index = jnp.arange(blocks, dtype=jnp.int32)
    first_flags = (block_index == 0).astype(jnp.float32)
    last_flags = (block_index == blocks - 1).astype(jnp.float32)

    def system(hamiltonian_block, lesser_block, greater_block, first_flag, last_flag):
        onsite = 0.5 * (hamiltonian_block + hamiltonian_block.T)
        matrix_real = energy_value[:, None, None] * identity - onsite - 0.5 * (greater_block[:, 0] - lesser_block[:, 0])
        matrix_imag = broadening * identity - 0.5 * (greater_block[:, 1] - lesser_block[:, 1])
        matrix_imag = matrix_imag + 0.5 * first_flag * gamma_left
        matrix_imag = matrix_imag + 0.5 * last_flag * gamma_right
        source_imag = lesser_block[:, 1] + first_flag * filling[:, 0, None, None] * gamma_left
        source_imag = source_imag + last_flag * filling[:, 1, None, None] * gamma_right
        return ((matrix_real, matrix_imag), (lesser_block[:, 0], source_imag))

    def forward(boundary, inputs):
        hamiltonian_block, link_block, lesser_block, greater_block, first_flag, last_flag = inputs
        matrix, source = system(hamiltonian_block, lesser_block, greater_block, first_flag, last_flag)
        matrix = (matrix[0] - pad_first(boundary[0], orbitals), matrix[1] - pad_first(boundary[1], orbitals))
        source = (source[0] + pad_first(boundary[2], orbitals), source[1] + pad_first(boundary[3], orbitals))
        green_block = inverted(matrix)
        lesser_green = complex_product(complex_product(green_block, source), adjoint(green_block))
        corners = jnp.stack([green_block[0][..., -interface:, -interface:], green_block[1][..., -interface:, -interface:], lesser_green[0][..., -interface:, -interface:], lesser_green[1][..., -interface:, -interface:]])
        next_boundary = matmul_high(transposed(link_block), matmul_high(corners, link_block))
        return (next_boundary, jnp.stack([green_block[0], green_block[1], lesser_green[0], lesser_green[1]]))
    start = jnp.zeros((4, energies, interface, interface), jnp.float32)
    _, forward_store = lax.scan(forward, start, (hamiltonian, coupling, lesser_all, greater_all, first_flags, last_flags))

    def backward(corner, inputs):
        saved, link_block = inputs
        green_block = (saved[0], saved[1])
        lesser_block = (saved[2], saved[3])
        coupled_all = matmul_high(link_block, matmul_high(corner, transposed(link_block)))
        coupled = (coupled_all[0], coupled_all[1])
        coupled_lesser = (coupled_all[2], coupled_all[3])
        column = (green_block[0][..., -interface:], green_block[1][..., -interface:])
        green_row = (green_block[0][..., -interface:, :], green_block[1][..., -interface:, :])
        lesser_column = (lesser_block[0][..., -interface:], lesser_block[1][..., -interface:])
        lesser_row = (lesser_block[0][..., -interface:, :], lesser_block[1][..., -interface:, :])
        weighted = complex_product(column, coupled)
        column_adjoint = adjoint(column)
        update = complex_product(weighted, green_row)
        full_green = (green_block[0] + update[0], green_block[1] + update[1])
        first_term = complex_product(complex_product(column, coupled_lesser), column_adjoint)
        second_term = complex_product(weighted, lesser_row)
        third_term = complex_product(lesser_column, complex_product(adjoint(coupled), column_adjoint))
        full_lesser = (lesser_block[0] + first_term[0] + second_term[0] + third_term[0], lesser_block[1] + first_term[1] + second_term[1] + third_term[1])
        new_corner = jnp.stack([full_green[0][..., :interface, :interface], full_green[1][..., :interface, :interface], full_lesser[0][..., :interface, :interface], full_lesser[1][..., :interface, :interface]])
        return (new_corner, jnp.stack([full_green[0], full_green[1], full_lesser[0], full_lesser[1]]))
    _, final_store = lax.scan(backward, start, (forward_store, coupling), reverse=True)
    green_real = final_store[:, 0]
    green_imag = final_store[:, 1]
    lesser_real = final_store[:, 2]
    lesser_imag = final_store[:, 3]
    greater_real = lesser_real + green_real - transposed(green_real)
    greater_imag = lesser_imag + green_imag + transposed(green_imag)
    amount = phonon_shift[0]

    def shifted(field, offset):
        rolled = jnp.roll(field, offset, axis=1)
        source_index = energy_index - offset
        valid_mask = ((source_index >= 0) & (source_index < energies)).astype(jnp.float32)
        return rolled * valid_mask[None, :, None, None]
    lesser_out_real = phonon_strength * ((phonon_bose + 1.0) * shifted(lesser_real, -amount) + phonon_bose * shifted(lesser_real, amount))
    lesser_out_imag = phonon_strength * ((phonon_bose + 1.0) * shifted(lesser_imag, -amount) + phonon_bose * shifted(lesser_imag, amount))
    greater_out_real = phonon_strength * ((phonon_bose + 1.0) * shifted(greater_real, amount) + phonon_bose * shifted(greater_real, -amount))
    greater_out_imag = phonon_strength * ((phonon_bose + 1.0) * shifted(greater_imag, amount) + phonon_bose * shifted(greater_imag, -amount))
    lesser_out = jnp.swapaxes(jnp.stack([lesser_out_real, lesser_out_imag], 2), 0, 1).reshape(lesser_in.shape)
    greater_out = jnp.swapaxes(jnp.stack([greater_out_real, greater_out_imag], 2), 0, 1).reshape(greater_in.shape)
    return (lesser_out, greater_out)
```

```python
import functools

import jax
import jax.numpy as jnp
from jax import lax
from jax.experimental import pallas as pl
from jax.experimental.pallas import tpu as pltpu
from jax.sharding import PartitionSpec as P

QUANTUM_BITS = 6


highest = lax.Precision.HIGHEST
broadening = 0.2
phonon_bose = 0.4
phonon_strength = 0.5


def shifted(value, axis, steps):
    count = lax.axis_size(axis)
    leading, last = (max(0, -steps), min(count, count - steps))
    return lax.ppermute(value, axis, [(source, source + steps) for source in range(leading, last)])


def from_behind(value, axis, steps):
    count = lax.axis_size(axis)
    pairs = [(source, (source + steps) % count) for source in range(count)]
    return lax.ppermute(value, axis, pairs)


def matmul_high(first_factor, second_factor):
    return jnp.matmul(first_factor, second_factor, precision=highest)


def transposed(matrix):
    return jnp.swapaxes(matrix, -1, -2)


def complex_product(first_pair, second_pair):
    return (
        matmul_high(first_pair[0], second_pair[0]) - matmul_high(first_pair[1], second_pair[1]),
        matmul_high(first_pair[0], second_pair[1]) + matmul_high(first_pair[1], second_pair[0]),
    )


def adjoint(complex_pair):
    return (transposed(complex_pair[0]), -transposed(complex_pair[1]))


def inverted(complex_pair):
    real_part, imag_part = complex_pair
    orbitals = real_part.shape[-1]
    normal_real = matmul_high(transposed(real_part), real_part) + matmul_high(
        transposed(imag_part), imag_part
    )
    normal_imag = matmul_high(transposed(real_part), imag_part) - matmul_high(
        transposed(imag_part), real_part
    )
    stacked = jnp.concatenate(
        [
            jnp.concatenate([normal_real, -normal_imag], -1),
            jnp.concatenate([normal_imag, normal_real], -1),
        ],
        -2,
    )
    factor = jnp.linalg.cholesky(stacked)
    right_side = jnp.concatenate([transposed(real_part), -transposed(imag_part)], -2)
    middle = lax.linalg.triangular_solve(factor, right_side, left_side=True, lower=True)
    solved = lax.linalg.triangular_solve(
        factor, middle, left_side=True, lower=True, transpose_a=True
    )
    return (solved[..., :orbitals, :], solved[..., orbitals:, :])


def pad_first(corner, orbitals):
    extra = orbitals - corner.shape[-1]
    return jnp.pad(corner, ((0, 0), (0, extra), (0, extra)))


def pad_last(corner, orbitals):
    extra = orbitals - corner.shape[-1]
    return jnp.pad(corner, ((0, 0), (extra, 0), (extra, 0)))


def settle(runner, stored, inbound, outbound, active):
    return lax.cond(active, lambda: runner(inbound), lambda: (stored, outbound))


def pass_right(outbound):
    return shifted(outbound, "dom", 1)


def pass_left(outbound):
    return shifted(outbound, "dom", -1)


def on_device(
    hamiltonian, coupling, contact_rates, occupation, lesser_in, greater_in, phonon_shift
):
    dom_index = lax.axis_index("dom")
    dom_count = lax.axis_size("dom")
    energy_index = lax.axis_index("energy")
    energy_count = lax.axis_size("energy")
    local_energies = occupation.shape[0]
    local_blocks = hamiltonian.shape[0]
    orbitals = hamiltonian.shape[1]
    interface = coupling.shape[1]
    total_energies = local_energies * energy_count
    global_energy = jnp.arange(local_energies, dtype=jnp.int32) * energy_count + energy_index
    energy_value = -1.5 + 3.0 * global_energy.astype(jnp.float32) / (total_energies - 1)
    identity = jnp.eye(orbitals, dtype=jnp.float32)
    extra = orbitals - interface
    gamma_left = jnp.pad(jnp.diag(contact_rates[0]), ((0, extra), (0, extra)))
    last_coupling = coupling[local_blocks - 1]
    gamma_right = jnp.pad(
        matmul_high(last_coupling * contact_rates[1][None, :], transposed(last_coupling)),
        ((extra, 0), (extra, 0)),
    )
    at_left = (dom_index == 0).astype(jnp.float32)
    at_right = (dom_index == dom_count - 1).astype(jnp.float32)

    def system(position):
        onsite = 0.5 * (hamiltonian[position] + hamiltonian[position].T)
        lesser_block = lesser_in[:, 0, position]
        greater_block = greater_in[:, 0, position]
        matrix_real = (
            energy_value[:, None, None] * identity
            - onsite
            - 0.5 * (greater_block[:, 0] - lesser_block[:, 0])
        )
        matrix_imag = broadening * identity - 0.5 * (greater_block[:, 1] - lesser_block[:, 1])
        source_imag = lesser_block[:, 1]
        matrix_imag = matrix_imag + 0.5 * at_left * gamma_left
        source_imag = source_imag + at_left * occupation[:, 0, 0, None, None] * gamma_left
        matrix_imag = matrix_imag + 0.5 * at_right * gamma_right
        source_imag = source_imag + at_right * occupation[:, 0, 1, None, None] * gamma_right
        return ((matrix_real, matrix_imag), (lesser_block[:, 0], source_imag))

    def trailing(green_block, lesser_block):
        return jnp.stack(
            [
                green_block[0][..., -interface:, -interface:],
                green_block[1][..., -interface:, -interface:],
                lesser_block[0][..., -interface:, -interface:],
                lesser_block[1][..., -interface:, -interface:],
            ]
        )

    def leading(green_block, lesser_block):
        return jnp.stack(
            [
                green_block[0][..., :interface, :interface],
                green_block[1][..., :interface, :interface],
                lesser_block[0][..., :interface, :interface],
                lesser_block[1][..., :interface, :interface],
            ]
        )

    def left_sweep(inbound):
        boundary = inbound
        matrix, source = system(0)
        matrix = (
            matrix[0] - pad_first(boundary[0], orbitals),
            matrix[1] - pad_first(boundary[1], orbitals),
        )
        source = (
            source[0] + pad_first(boundary[2], orbitals),
            source[1] + pad_first(boundary[3], orbitals),
        )
        green_block = inverted(matrix)
        lesser_block = complex_product(complex_product(green_block, source), adjoint(green_block))
        kept_blocks = [boundary]
        link_block = coupling[0]
        boundary = matmul_high(
            transposed(link_block), matmul_high(trailing(green_block, lesser_block), link_block)
        )
        return (jnp.stack(kept_blocks, 2), boundary)

    def right_sweep(inbound):
        corner = inbound
        kept_blocks = [None] * local_blocks
        for position in reversed(range(local_blocks)):
            link_block = coupling[position]
            boundary = matmul_high(link_block, matmul_high(corner, transposed(link_block)))
            matrix, source = system(position)
            matrix = (
                matrix[0] - pad_last(boundary[0], orbitals),
                matrix[1] - pad_last(boundary[1], orbitals),
            )
            source = (
                source[0] + pad_last(boundary[2], orbitals),
                source[1] + pad_last(boundary[3], orbitals),
            )
            green_block = inverted(matrix)
            lesser_block = complex_product(
                complex_product(green_block, source), adjoint(green_block)
            )
            kept_blocks[position] = boundary
            corner = leading(green_block, lesser_block)
        return (jnp.stack(kept_blocks, 2), corner)

    def ascending(section_number):
        return section_number

    def descending(section_number):
        return dom_count - 1 - section_number

    zeros_out = jnp.zeros((4, local_energies, interface, interface), jnp.float32)
    zeros_bounds = jnp.zeros((4, local_energies, local_blocks, interface, interface), jnp.float32)

    def left_runner(inbound):
        return left_sweep(inbound)

    runners = [left_runner, right_sweep]
    orderings = [ascending, descending]
    senders = [pass_right, pass_left]
    stores = [zeros_bounds, zeros_bounds]
    outbounds = [zeros_out, zeros_out]

    def advance(section_number, stores, inbounds, outbounds):
        new_stores = []
        new_outbounds = []
        for chain_number in range(len(runners)):
            active = dom_index == orderings[chain_number](section_number)
            settled = settle(
                runners[chain_number],
                stores[chain_number],
                inbounds[chain_number],
                outbounds[chain_number],
                active,
            )
            new_stores.append(settled[0])
            new_outbounds.append(settled[1])
        return (new_stores, new_outbounds)

    def turn(section_number, loop_state):
        stores, inbounds, outbounds = loop_state
        stores, outbounds = advance(section_number, stores, inbounds, outbounds)
        inbounds = [
            senders[chain_number](outbounds[chain_number]) for chain_number in range(len(runners))
        ]
        return (stores, inbounds, outbounds)

    inbounds = [jnp.zeros_like(outbound) for outbound in outbounds]
    stores, inbounds, outbounds = lax.fori_loop(
        0, dom_count - 1, turn, (stores, inbounds, outbounds)
    )
    stores, outbounds = advance(dom_count - 1, stores, inbounds, outbounds)
    left_store, right_store = stores
    position = 0
    left_part = left_store[:, :, position]
    right_part = right_store[:, :, position]
    matrix, source = system(position)
    matrix = (
        matrix[0] - pad_first(left_part[0], orbitals) - pad_last(right_part[0], orbitals),
        matrix[1] - pad_first(left_part[1], orbitals) - pad_last(right_part[1], orbitals),
    )
    source = (
        source[0] + pad_first(left_part[2], orbitals) + pad_last(right_part[2], orbitals),
        source[1] + pad_first(left_part[3], orbitals) + pad_last(right_part[3], orbitals),
    )
    green_block = inverted(matrix)
    lesser_block = complex_product(complex_product(green_block, source), adjoint(green_block))
    kept_final = [jnp.stack([green_block[0], green_block[1], lesser_block[0], lesser_block[1]])]
    final_store = jnp.stack(kept_final, 2)
    green_real = final_store[0]
    green_imag = final_store[1]
    lesser_real = final_store[2]
    lesser_imag = final_store[3]
    greater_real = lesser_real + green_real - transposed(green_real)
    greater_imag = lesser_imag + green_imag + transposed(green_imag)
    shift_amount = phonon_shift[0]
    quantum_limit = min(2**QUANTUM_BITS, total_energies // 2)
    bit_count = (quantum_limit - 1).bit_length()

    def moved_by(payload, direction):
        for bit_number in range(bit_count):
            amount = direction * 2**bit_number
            remainder = amount % energy_count
            carried = amount // energy_count
            arrived = from_behind(payload, "energy", remainder)
            aligned = jnp.where(
                energy_index < remainder,
                jnp.roll(arrived, carried + 1, axis=1),
                jnp.roll(arrived, carried, axis=1),
            )
            chosen = jnp.right_shift(shift_amount, bit_number) & 1 == 1
            payload = jnp.where(chosen, aligned, payload)
        return payload

    payload = jnp.stack([lesser_real, lesser_imag, greater_real, greater_imag])
    below = moved_by(payload, 1)
    above = moved_by(payload, -1)
    below_lesser = (below[0], below[1])
    below_greater = (below[2], below[3])
    above_lesser = (above[0], above[1])
    above_greater = (above[2], above[3])
    below_source = global_energy - shift_amount
    above_source = global_energy + shift_amount
    valid_below = ((below_source >= 0) & (below_source < total_energies)).astype(jnp.float32)[
        :, None, None, None
    ]
    valid_above = ((above_source >= 0) & (above_source < total_energies)).astype(jnp.float32)[
        :, None, None, None
    ]
    lesser_out_real = phonon_strength * (
        (phonon_bose + 1.0) * (above_lesser[0] * valid_above)
        + phonon_bose * (below_lesser[0] * valid_below)
    )
    lesser_out_imag = phonon_strength * (
        (phonon_bose + 1.0) * (above_lesser[1] * valid_above)
        + phonon_bose * (below_lesser[1] * valid_below)
    )
    greater_out_real = phonon_strength * (
        (phonon_bose + 1.0) * (below_greater[0] * valid_below)
        + phonon_bose * (above_greater[0] * valid_above)
    )
    greater_out_imag = phonon_strength * (
        (phonon_bose + 1.0) * (below_greater[1] * valid_below)
        + phonon_bose * (above_greater[1] * valid_above)
    )
    lesser_out = jnp.stack([lesser_out_real, lesser_out_imag], 2)[:, None]
    greater_out = jnp.stack([greater_out_real, greater_out_imag], 2)[:, None]
    return (lesser_out, greater_out)


ROWS_BY_ROWS = (((1,), (1,)), ((), ()))
ROWS_BY_COLUMNS = (((1,), (0,)), ((), ()))


def dot(first, second, dims=ROWS_BY_COLUMNS):
    return lax.dot_general(
        first, second, dims, precision=highest, preferred_element_type=jnp.float32
    )


def lanes_of(array):
    return lax.broadcasted_iota(jnp.int32, array.shape, 1)


def times_i(wide):
    half = wide.shape[1] // 2
    moved = pltpu.roll(wide, half, 1)
    return jnp.where(lanes_of(wide) < half, -moved, moved)


def embedded(wide):
    return jnp.concatenate([wide, times_i(wide)], 0)


def wide_product(first, second):
    return dot(first, embedded(second))


def wide_product_adjoint(first, second):
    return dot(first, embedded(second), ROWS_BY_ROWS)


def twice_diagonal(matrix):
    zero = jnp.zeros_like(matrix)
    return jnp.concatenate(
        [jnp.concatenate([matrix, zero], 1), jnp.concatenate([zero, matrix], 1)], 0
    )


def sandwiched(matrix, wide):
    return dot(dot(matrix, wide), twice_diagonal(matrix), ROWS_BY_ROWS)


def wide_inverse(wide):
    size = wide.shape[0]
    rows = lax.broadcasted_iota(jnp.int32, wide.shape, 0)
    lanes = lanes_of(wide)
    row_lanes = lax.broadcasted_iota(jnp.int32, (1, wide.shape[1]), 1)
    for step in range(size):
        row = wide[step : step + 1, :]
        pivot_real = jnp.broadcast_to(row[:, step : step + 1], row.shape)
        pivot_imag = jnp.broadcast_to(row[:, size + step : size + step + 1], row.shape)
        scale = 1.0 / (pivot_real * pivot_real + pivot_imag * pivot_imag)
        row = jnp.where(row_lanes == step, 1.0, jnp.where(row_lanes == size + step, 0.0, row))
        row = (pivot_real * row - pivot_imag * times_i(row)) * scale
        turned = times_i(row)
        column_real = jnp.broadcast_to(wide[:, step : step + 1], wide.shape)
        column_imag = jnp.broadcast_to(wide[:, size + step : size + step + 1], wide.shape)
        at_row = rows == step
        column_real = jnp.where(at_row, -1.0, column_real)
        column_imag = jnp.where(at_row, 0.0, column_imag)
        cleared = at_row | (lanes == step) | (lanes == size + step)
        wide = jnp.where(cleared, 0.0, wide) - column_real * row - column_imag * turned
    return wide


def flipped(flag, matrix):
    half = matrix.shape[0] // 2
    moved = pltpu.roll(matrix, half, 1)
    moved = jnp.concatenate([moved[half:], moved[:half]], 0)
    return jnp.where(flag, moved, matrix)


def wide_quarters(real, imag):
    half = real.shape[0] // 2
    left_lanes = lax.broadcasted_iota(jnp.int32, (half, 2 * half), 1) < half
    quarters = []
    for start in (0, half):
        real_rows, imag_rows = real[start : start + half], imag[start : start + half]
        quarters.append(jnp.where(left_lanes, real_rows, pltpu.roll(imag_rows, half, 1)))
        quarters.append(jnp.where(left_lanes, pltpu.roll(real_rows, half, 1), imag_rows))
    return quarters


def real_imag_rows(left, right):
    half = left.shape[0]
    left_lanes = lanes_of(left) < half
    return (
        jnp.where(left_lanes, left, pltpu.roll(right, half, 1)),
        jnp.where(left_lanes, pltpu.roll(left, half, 1), right),
    )


def unit(size):
    rows = lax.broadcasted_iota(jnp.int32, (size, size), 0)
    return (rows == lax.broadcasted_iota(jnp.int32, (size, size), 1)).astype(jnp.float32)


def eliminate_kernel(
    place, numbers, hamiltonian, coupling, rates, lesser, greater, send, kept, source
):
    flag = place[0] == 1
    orbitals = hamiltonian.shape[0]
    half = coupling.shape[0]
    identity = unit(orbitals)
    link = coupling[...]
    system_real = (
        numbers[0] * identity
        - 0.5 * (hamiltonian[...] + hamiltonian[...].T)
        - 0.5 * (greater[0] - lesser[0])
    )
    system_imag = broadening * identity - 0.5 * (greater[1] - lesser[1])
    system_real = flipped(flag, system_real)
    system_imag = flipped(flag, system_imag)
    source_real = flipped(flag, lesser[0])
    source_imag = flipped(flag, lesser[1])
    small = unit(half)
    left_gamma = small * rates[0:1, :]
    right_gamma = dot(link * rates[1:2, :], link, ROWS_BY_ROWS)
    gamma = jnp.where(flag, right_gamma, left_gamma)
    zero = jnp.zeros_like(gamma)
    gamma_turned = jnp.concatenate([zero, gamma], 1)
    inner, upper, lower, outer = wide_quarters(system_real, system_imag)
    inner = inner + 0.5 * gamma_turned
    filling = jnp.where(flag, numbers[2], numbers[1])
    gamma_padded = jnp.concatenate([gamma, zero], 1)
    source_imag = source_imag + filling * jnp.concatenate(
        [gamma_padded, jnp.zeros_like(gamma_padded)], 0
    )
    inverse = wide_inverse(inner)
    right = wide_product(inverse, upper)
    left = wide_product(lower, inverse)
    schur = outer - wide_product(left, upper)
    kept[0] = inverse
    kept[1] = right
    kept[2] = left
    kept[3] = schur
    source[:, :orbitals] = source_real
    source[:, orbitals:] = source_imag
    first, above, below, last = wide_quarters(source_real, source_imag)
    reduced = last - wide_product(left, above) - wide_product_adjoint(below, left)
    reduced = reduced + wide_product_adjoint(wide_product(left, first), left)
    corner = wide_inverse(schur)
    corner_lesser = wide_product_adjoint(wide_product(corner, reduced), corner)
    outgoing = jnp.where(flag, small, link.T)
    send[0] = sandwiched(outgoing, corner)
    send[1] = sandwiched(outgoing, corner_lesser)


def packed(real, imag):
    rows = lax.broadcasted_iota(jnp.int32, real.shape, 0)
    return jnp.where(rows > lanes_of(real), real, imag)


def complete_kernel(place, arrived, kept, source, coupling, payload):
    flag = place[0] == 1
    half = coupling.shape[0]
    orbitals = 2 * half
    incoming = jnp.where(flag, unit(half), coupling[...])
    boundary = sandwiched(incoming, arrived[0])
    boundary_lesser = sandwiched(incoming, arrived[1])
    inverse, right, left = kept[0], kept[1], kept[2]
    last = wide_inverse(kept[3] - boundary)
    lower = wide_product(last, left)
    upper = -wide_product(right, last)
    inner = inverse + wide_product(right, lower)
    top_real, top_imag = real_imag_rows(inner, upper)
    bottom_real, bottom_imag = real_imag_rows(-lower, last)
    green_real = jnp.concatenate([top_real, bottom_real], 0)
    green_imag = jnp.concatenate([top_imag, bottom_imag], 0)
    green = jnp.concatenate([green_real, green_imag], 1)
    added_real, added_imag = real_imag_rows(jnp.zeros_like(boundary_lesser), boundary_lesser)
    source_bottom = source[half:, :] + jnp.concatenate([added_real, added_imag], 1)
    sources = jnp.concatenate([source[:half, :], source_bottom], 0)
    lesser = wide_product_adjoint(wide_product(green, sources), green)
    lesser_real = flipped(flag, lesser[:, :orbitals])
    lesser_imag = flipped(flag, lesser[:, orbitals:])
    spectral_real = flipped(flag, green_real - green_real.T)
    spectral_imag = flipped(flag, green_imag + green_imag.T)
    payload[0] = packed(lesser_real, lesser_imag)
    payload[1] = packed(lesser_real + spectral_real, lesser_imag + spectral_imag)


def combine_kernel(below, above, lesser_out, greater_out):
    emitted = phonon_strength * (phonon_bose + 1.0)
    absorbed = phonon_strength * phonon_bose
    for out, mixed in (
        (lesser_out, emitted * above[0] + absorbed * below[0]),
        (greater_out, emitted * below[1] + absorbed * above[1]),
    ):
        rows = lax.broadcasted_iota(jnp.int32, mixed.shape, 0)
        lanes = lanes_of(mixed)
        mirrored = mixed.T
        out[0] = jnp.where(rows > lanes, mixed, jnp.where(rows < lanes, -mirrored, 0.0))
        out[1] = jnp.where(rows > lanes, mirrored, mixed)


def vmem(count):
    return [pl.BlockSpec(memory_space=pltpu.VMEM)] * count


def smem(count):
    return [pl.BlockSpec(memory_space=pltpu.SMEM)] * count


def on_pair(hamiltonian, coupling, contact_rates, occupation, lesser_in, greater_in, phonon_shift):
    energy_index = lax.axis_index("energy")
    energy_count = lax.axis_size("energy")
    orbitals = hamiltonian.shape[1]
    half = coupling.shape[1]
    energy_value = -1.5 + 3.0 * energy_index.astype(jnp.float32) / (energy_count - 1)
    numbers = jnp.concatenate([energy_value[None], occupation[0, 0]])
    place = lax.axis_index("dom").astype(jnp.int32)[None]
    wide = jax.ShapeDtypeStruct((4, half, orbitals), jnp.float32)
    send, kept, source = pl.pallas_call(
        eliminate_kernel,
        out_shape=(
            jax.ShapeDtypeStruct((2, half, orbitals), jnp.float32),
            wide,
            jax.ShapeDtypeStruct((orbitals, 2 * orbitals), jnp.float32),
        ),
        in_specs=smem(2) + vmem(5),
        out_specs=tuple(vmem(3)),
    )(
        place,
        numbers,
        hamiltonian[0],
        coupling[0],
        contact_rates,
        lesser_in[0, 0, 0],
        greater_in[0, 0, 0],
    )
    arrived = lax.ppermute(send, "dom", [(0, 1), (1, 0)])
    payload = pl.pallas_call(
        complete_kernel,
        out_shape=jax.ShapeDtypeStruct((2, orbitals, orbitals), jnp.float32),
        in_specs=smem(1) + vmem(4),
        out_specs=vmem(1)[0],
    )(place, arrived, kept, source, coupling[0])

    def moved(steps, value):
        count = energy_count - steps
        upward = [(start, start + steps) for start in range(count)]
        downward = [(start + steps, start) for start in range(count)]
        return (lax.ppermute(value, "energy", upward), lax.ppermute(value, "energy", downward))

    limit = min(2**QUANTUM_BITS, energy_count // 2)
    below, above = lax.switch(
        phonon_shift[0] - 1,
        [functools.partial(moved, steps) for steps in range(1, max(limit, 2))],
        payload,
    )
    block = jax.ShapeDtypeStruct((2, orbitals, orbitals), jnp.float32)
    outs = pl.pallas_call(
        combine_kernel, out_shape=(block, block), in_specs=vmem(2), out_specs=tuple(vmem(2))
    )(below, above)
    return tuple(out[None, None, None] for out in outs)


def choose(hamiltonian, coupling, contact_rates, occupation, lesser_in, greater_in, phonon_shift):
    pair = lax.axis_size("dom") == 2 and hamiltonian.shape[0] == 1 and occupation.shape[0] == 1
    lanes_fit = hamiltonian.shape[1] == 2 * coupling.shape[1] and hamiltonian.shape[1] % 128 == 0
    program = on_pair if pair and lanes_fit else on_device
    return program(
        hamiltonian, coupling, contact_rates, occupation, lesser_in, greater_in, phonon_shift
    )


def solution(mesh):
    return jax.shard_map(
        choose,
        mesh=mesh,
        in_specs=(
            P("dom", None, None),
            P("dom", None, None),
            P(),
            P(None, "energy", None),
            P(None, "energy", "dom", None, None, None),
            P(None, "energy", "dom", None, None, None),
            P(),
        ),
        out_specs=(
            P(None, "energy", "dom", None, None, None),
            P(None, "energy", "dom", None, None, None),
        ),
        check_vma=False,
    )
```

```python
import functools

import jax
import jax.numpy as jnp
from jax import lax
from jax.experimental import pallas as pl
from jax.experimental.pallas import tpu as pltpu
from jax.sharding import PartitionSpec as P

QUANTUM_BITS = 6


highest = lax.Precision.HIGHEST
broadening = 0.2
phonon_bose = 0.4
phonon_strength = 0.5


def shifted(value, axis, steps):
    count = lax.axis_size(axis)
    leading, last = (max(0, -steps), min(count, count - steps))
    return lax.ppermute(value, axis, [(source, source + steps) for source in range(leading, last)])


def from_behind(value, axis, steps):
    count = lax.axis_size(axis)
    pairs = [(source, (source + steps) % count) for source in range(count)]
    return lax.ppermute(value, axis, pairs)


def matmul_high(first_factor, second_factor):
    return jnp.matmul(first_factor, second_factor, precision=highest)


def transposed(matrix):
    return jnp.swapaxes(matrix, -1, -2)


def complex_product(first_pair, second_pair):
    return (
        matmul_high(first_pair[0], second_pair[0]) - matmul_high(first_pair[1], second_pair[1]),
        matmul_high(first_pair[0], second_pair[1]) + matmul_high(first_pair[1], second_pair[0]),
    )


def adjoint(complex_pair):
    return (transposed(complex_pair[0]), -transposed(complex_pair[1]))


def inverted(complex_pair):
    real_part, imag_part = complex_pair
    orbitals = real_part.shape[-1]
    normal_real = matmul_high(transposed(real_part), real_part) + matmul_high(
        transposed(imag_part), imag_part
    )
    normal_imag = matmul_high(transposed(real_part), imag_part) - matmul_high(
        transposed(imag_part), real_part
    )
    stacked = jnp.concatenate(
        [
            jnp.concatenate([normal_real, -normal_imag], -1),
            jnp.concatenate([normal_imag, normal_real], -1),
        ],
        -2,
    )
    factor = jnp.linalg.cholesky(stacked)
    right_side = jnp.concatenate([transposed(real_part), -transposed(imag_part)], -2)
    middle = lax.linalg.triangular_solve(factor, right_side, left_side=True, lower=True)
    solved = lax.linalg.triangular_solve(
        factor, middle, left_side=True, lower=True, transpose_a=True
    )
    return (solved[..., :orbitals, :], solved[..., orbitals:, :])


def pad_first(corner, orbitals):
    extra = orbitals - corner.shape[-1]
    return jnp.pad(corner, ((0, 0), (0, extra), (0, extra)))


def pad_last(corner, orbitals):
    extra = orbitals - corner.shape[-1]
    return jnp.pad(corner, ((0, 0), (extra, 0), (extra, 0)))


def settle(runner, stored, inbound, outbound, active):
    return lax.cond(active, lambda: runner(inbound), lambda: (stored, outbound))


def pass_right(outbound):
    return shifted(outbound, "dom", 1)


def pass_left(outbound):
    return shifted(outbound, "dom", -1)


def on_device(
    hamiltonian, coupling, contact_rates, occupation, lesser_in, greater_in, phonon_shift
):
    dom_index = lax.axis_index("dom")
    dom_count = lax.axis_size("dom")
    energy_index = lax.axis_index("energy")
    energy_count = lax.axis_size("energy")
    local_energies = occupation.shape[0]
    local_blocks = hamiltonian.shape[0]
    orbitals = hamiltonian.shape[1]
    interface = coupling.shape[1]
    total_energies = local_energies * energy_count
    global_energy = jnp.arange(local_energies, dtype=jnp.int32) * energy_count + energy_index
    energy_value = -1.5 + 3.0 * global_energy.astype(jnp.float32) / (total_energies - 1)
    identity = jnp.eye(orbitals, dtype=jnp.float32)
    extra = orbitals - interface
    gamma_left = jnp.pad(jnp.diag(contact_rates[0]), ((0, extra), (0, extra)))
    last_coupling = coupling[local_blocks - 1]
    gamma_right = jnp.pad(
        matmul_high(last_coupling * contact_rates[1][None, :], transposed(last_coupling)),
        ((extra, 0), (extra, 0)),
    )
    at_left = (dom_index == 0).astype(jnp.float32)
    at_right = (dom_index == dom_count - 1).astype(jnp.float32)

    def system(position):
        onsite = 0.5 * (hamiltonian[position] + hamiltonian[position].T)
        lesser_block = lesser_in[:, 0, position]
        greater_block = greater_in[:, 0, position]
        matrix_real = (
            energy_value[:, None, None] * identity
            - onsite
            - 0.5 * (greater_block[:, 0] - lesser_block[:, 0])
        )
        matrix_imag = broadening * identity - 0.5 * (greater_block[:, 1] - lesser_block[:, 1])
        source_imag = lesser_block[:, 1]
        matrix_imag = matrix_imag + 0.5 * at_left * gamma_left
        source_imag = source_imag + at_left * occupation[:, 0, 0, None, None] * gamma_left
        matrix_imag = matrix_imag + 0.5 * at_right * gamma_right
        source_imag = source_imag + at_right * occupation[:, 0, 1, None, None] * gamma_right
        return ((matrix_real, matrix_imag), (lesser_block[:, 0], source_imag))

    def trailing(green_block, lesser_block):
        return jnp.stack(
            [
                green_block[0][..., -interface:, -interface:],
                green_block[1][..., -interface:, -interface:],
                lesser_block[0][..., -interface:, -interface:],
                lesser_block[1][..., -interface:, -interface:],
            ]
        )

    def leading(green_block, lesser_block):
        return jnp.stack(
            [
                green_block[0][..., :interface, :interface],
                green_block[1][..., :interface, :interface],
                lesser_block[0][..., :interface, :interface],
                lesser_block[1][..., :interface, :interface],
            ]
        )

    def left_sweep(inbound):
        boundary = inbound
        matrix, source = system(0)
        matrix = (
            matrix[0] - pad_first(boundary[0], orbitals),
            matrix[1] - pad_first(boundary[1], orbitals),
        )
        source = (
            source[0] + pad_first(boundary[2], orbitals),
            source[1] + pad_first(boundary[3], orbitals),
        )
        green_block = inverted(matrix)
        lesser_block = complex_product(complex_product(green_block, source), adjoint(green_block))
        kept_blocks = [boundary]
        link_block = coupling[0]
        boundary = matmul_high(
            transposed(link_block), matmul_high(trailing(green_block, lesser_block), link_block)
        )
        return (jnp.stack(kept_blocks, 2), boundary)

    def right_sweep(inbound):
        corner = inbound
        kept_blocks = [None] * local_blocks
        for position in reversed(range(local_blocks)):
            link_block = coupling[position]
            boundary = matmul_high(link_block, matmul_high(corner, transposed(link_block)))
            matrix, source = system(position)
            matrix = (
                matrix[0] - pad_last(boundary[0], orbitals),
                matrix[1] - pad_last(boundary[1], orbitals),
            )
            source = (
                source[0] + pad_last(boundary[2], orbitals),
                source[1] + pad_last(boundary[3], orbitals),
            )
            green_block = inverted(matrix)
            lesser_block = complex_product(
                complex_product(green_block, source), adjoint(green_block)
            )
            kept_blocks[position] = boundary
            corner = leading(green_block, lesser_block)
        return (jnp.stack(kept_blocks, 2), corner)

    def ascending(section_number):
        return section_number

    def descending(section_number):
        return dom_count - 1 - section_number

    zeros_out = jnp.zeros((4, local_energies, interface, interface), jnp.float32)
    zeros_bounds = jnp.zeros((4, local_energies, local_blocks, interface, interface), jnp.float32)

    def left_runner(inbound):
        return left_sweep(inbound)

    runners = [left_runner, right_sweep]
    orderings = [ascending, descending]
    senders = [pass_right, pass_left]
    stores = [zeros_bounds, zeros_bounds]
    outbounds = [zeros_out, zeros_out]

    def advance(section_number, stores, inbounds, outbounds):
        new_stores = []
        new_outbounds = []
        for chain_number in range(len(runners)):
            active = dom_index == orderings[chain_number](section_number)
            settled = settle(
                runners[chain_number],
                stores[chain_number],
                inbounds[chain_number],
                outbounds[chain_number],
                active,
            )
            new_stores.append(settled[0])
            new_outbounds.append(settled[1])
        return (new_stores, new_outbounds)

    def turn(section_number, loop_state):
        stores, inbounds, outbounds = loop_state
        stores, outbounds = advance(section_number, stores, inbounds, outbounds)
        inbounds = [
            senders[chain_number](outbounds[chain_number]) for chain_number in range(len(runners))
        ]
        return (stores, inbounds, outbounds)

    inbounds = [jnp.zeros_like(outbound) for outbound in outbounds]
    stores, inbounds, outbounds = lax.fori_loop(
        0, dom_count - 1, turn, (stores, inbounds, outbounds)
    )
    stores, outbounds = advance(dom_count - 1, stores, inbounds, outbounds)
    left_store, right_store = stores
    position = 0
    left_part = left_store[:, :, position]
    right_part = right_store[:, :, position]
    matrix, source = system(position)
    matrix = (
        matrix[0] - pad_first(left_part[0], orbitals) - pad_last(right_part[0], orbitals),
        matrix[1] - pad_first(left_part[1], orbitals) - pad_last(right_part[1], orbitals),
    )
    source = (
        source[0] + pad_first(left_part[2], orbitals) + pad_last(right_part[2], orbitals),
        source[1] + pad_first(left_part[3], orbitals) + pad_last(right_part[3], orbitals),
    )
    green_block = inverted(matrix)
    lesser_block = complex_product(complex_product(green_block, source), adjoint(green_block))
    kept_final = [jnp.stack([green_block[0], green_block[1], lesser_block[0], lesser_block[1]])]
    final_store = jnp.stack(kept_final, 2)
    green_real = final_store[0]
    green_imag = final_store[1]
    lesser_real = final_store[2]
    lesser_imag = final_store[3]
    greater_real = lesser_real + green_real - transposed(green_real)
    greater_imag = lesser_imag + green_imag + transposed(green_imag)
    shift_amount = phonon_shift[0]
    quantum_limit = min(2**QUANTUM_BITS, total_energies // 2)
    bit_count = (quantum_limit - 1).bit_length()

    def moved_by(payload, direction):
        for bit_number in range(bit_count):
            amount = direction * 2**bit_number
            remainder = amount % energy_count
            carried = amount // energy_count
            arrived = from_behind(payload, "energy", remainder)
            aligned = jnp.where(
                energy_index < remainder,
                jnp.roll(arrived, carried + 1, axis=1),
                jnp.roll(arrived, carried, axis=1),
            )
            chosen = jnp.right_shift(shift_amount, bit_number) & 1 == 1
            payload = jnp.where(chosen, aligned, payload)
        return payload

    payload = jnp.stack([lesser_real, lesser_imag, greater_real, greater_imag])
    below = moved_by(payload, 1)
    above = moved_by(payload, -1)
    below_lesser = (below[0], below[1])
    below_greater = (below[2], below[3])
    above_lesser = (above[0], above[1])
    above_greater = (above[2], above[3])
    below_source = global_energy - shift_amount
    above_source = global_energy + shift_amount
    valid_below = ((below_source >= 0) & (below_source < total_energies)).astype(jnp.float32)[
        :, None, None, None
    ]
    valid_above = ((above_source >= 0) & (above_source < total_energies)).astype(jnp.float32)[
        :, None, None, None
    ]
    lesser_out_real = phonon_strength * (
        (phonon_bose + 1.0) * (above_lesser[0] * valid_above)
        + phonon_bose * (below_lesser[0] * valid_below)
    )
    lesser_out_imag = phonon_strength * (
        (phonon_bose + 1.0) * (above_lesser[1] * valid_above)
        + phonon_bose * (below_lesser[1] * valid_below)
    )
    greater_out_real = phonon_strength * (
        (phonon_bose + 1.0) * (below_greater[0] * valid_below)
        + phonon_bose * (above_greater[0] * valid_above)
    )
    greater_out_imag = phonon_strength * (
        (phonon_bose + 1.0) * (below_greater[1] * valid_below)
        + phonon_bose * (above_greater[1] * valid_above)
    )
    lesser_out = jnp.stack([lesser_out_real, lesser_out_imag], 2)[:, None]
    greater_out = jnp.stack([greater_out_real, greater_out_imag], 2)[:, None]
    return (lesser_out, greater_out)


ROWS_BY_ROWS = (((1,), (1,)), ((), ()))
ROWS_BY_COLUMNS = (((1,), (0,)), ((), ()))


def dot(first, second, dims=ROWS_BY_COLUMNS):
    return lax.dot_general(
        first, second, dims, precision=highest, preferred_element_type=jnp.float32
    )


def lanes_of(array):
    return lax.broadcasted_iota(jnp.int32, array.shape, 1)


def times_i(wide):
    half = wide.shape[1] // 2
    moved = pltpu.roll(wide, half, 1)
    return jnp.where(lanes_of(wide) < half, -moved, moved)


def embedded(wide):
    return jnp.concatenate([wide, times_i(wide)], 0)


def wide_product(first, second):
    return dot(first, embedded(second))


def wide_product_adjoint(first, second):
    return dot(first, embedded(second), ROWS_BY_ROWS)


def twice_diagonal(matrix):
    zero = jnp.zeros_like(matrix)
    return jnp.concatenate(
        [jnp.concatenate([matrix, zero], 1), jnp.concatenate([zero, matrix], 1)], 0
    )


def sandwiched(matrix, wide):
    return dot(dot(matrix, wide), twice_diagonal(matrix), ROWS_BY_ROWS)


def scaled_row(real, imag, row):
    plain, turned = row
    return (real * plain + imag * turned, real * turned - imag * plain)


def wide_inverse(wide, group=4):
    size = wide.shape[0]
    rows = lax.broadcasted_iota(jnp.int32, wide.shape, 0)
    lanes = lanes_of(wide)
    row_lanes = lax.broadcasted_iota(jnp.int32, (1, wide.shape[1]), 1)
    for start in range(0, size, group):
        members = range(group)
        in_lanes = (lanes >= start) & (lanes < start + group)
        in_lanes = in_lanes | ((lanes >= size + start) & (lanes < size + start + group))
        in_rows = (rows >= start) & (rows < start + group)
        picked = (row_lanes >= start) & (row_lanes < start + group)
        picked = picked | ((row_lanes >= size + start) & (row_lanes < size + start + group))
        corner, held = [], []
        for member in members:
            row = wide[start + member : start + member + 1, :]
            corner.append(
                [
                    tuple(
                        jnp.broadcast_to(row[:, lane : lane + 1], row.shape)
                        for lane in (start + other, size + start + other)
                    )
                    for other in members
                ]
            )
            turned = jnp.where(picked, 0.0, times_i(row))
            row = jnp.where(picked, 0.0, row)
            row = jnp.where(row_lanes == start + member, 1.0, row)
            turned = jnp.where(row_lanes == size + start + member, 1.0, turned)
            held.append((row, turned))
        for pivot in members:
            real, imag = corner[pivot][pivot]
            scale = 1.0 / (real * real + imag * imag)
            real, imag = real * scale, -imag * scale
            held[pivot] = scaled_row(real, imag, held[pivot])
            for other in range(pivot + 1, group):
                entry = corner[pivot][other]
                corner[pivot][other] = (
                    real * entry[0] - imag * entry[1],
                    real * entry[1] + imag * entry[0],
                )
            for member in members:
                if member == pivot:
                    continue
                real, imag = corner[member][pivot]
                for other in range(pivot + 1, group):
                    entry, kept = corner[pivot][other], corner[member][other]
                    corner[member][other] = (
                        kept[0] - (real * entry[0] - imag * entry[1]),
                        kept[1] - (real * entry[1] + imag * entry[0]),
                    )
                lost = scaled_row(real, imag, held[pivot])
                held[member] = (held[member][0] - lost[0], held[member][1] - lost[1])
        updated = jnp.where(in_rows | in_lanes, 0.0, wide)
        for member in members:
            lane = start + member
            column_real = jnp.broadcast_to(wide[:, lane : lane + 1], wide.shape)
            lane = size + lane
            column_imag = jnp.broadcast_to(wide[:, lane : lane + 1], wide.shape)
            at_member = (rows == start + member).astype(jnp.float32)
            column_real = jnp.where(in_rows, -at_member, column_real)
            column_imag = jnp.where(in_rows, 0.0, column_imag)
            updated = updated - column_real * held[member][0] - column_imag * held[member][1]
        wide = updated
    return wide


def flipped(flag, matrix):
    half = matrix.shape[0] // 2
    moved = pltpu.roll(matrix, half, 1)
    moved = jnp.concatenate([moved[half:], moved[:half]], 0)
    return jnp.where(flag, moved, matrix)


def wide_quarters(real, imag):
    half = real.shape[0] // 2
    left_lanes = lax.broadcasted_iota(jnp.int32, (half, 2 * half), 1) < half
    quarters = []
    for start in (0, half):
        real_rows, imag_rows = real[start : start + half], imag[start : start + half]
        quarters.append(jnp.where(left_lanes, real_rows, pltpu.roll(imag_rows, half, 1)))
        quarters.append(jnp.where(left_lanes, pltpu.roll(real_rows, half, 1), imag_rows))
    return quarters


def real_imag_rows(left, right):
    half = left.shape[0]
    left_lanes = lanes_of(left) < half
    return (
        jnp.where(left_lanes, left, pltpu.roll(right, half, 1)),
        jnp.where(left_lanes, pltpu.roll(left, half, 1), right),
    )


def unit(size):
    rows = lax.broadcasted_iota(jnp.int32, (size, size), 0)
    return (rows == lax.broadcasted_iota(jnp.int32, (size, size), 1)).astype(jnp.float32)


def eliminate_kernel(
    place, numbers, hamiltonian, coupling, rates, lesser, greater, send, kept, source
):
    flag = place[0] == 1
    orbitals = hamiltonian.shape[0]
    half = coupling.shape[0]
    identity = unit(orbitals)
    link = coupling[...]
    system_real = (
        numbers[0] * identity
        - 0.5 * (hamiltonian[...] + hamiltonian[...].T)
        - 0.5 * (greater[0] - lesser[0])
    )
    system_imag = broadening * identity - 0.5 * (greater[1] - lesser[1])
    system_real = flipped(flag, system_real)
    system_imag = flipped(flag, system_imag)
    source_real = flipped(flag, lesser[0])
    source_imag = flipped(flag, lesser[1])
    small = unit(half)
    left_gamma = small * rates[0:1, :]
    right_gamma = dot(link * rates[1:2, :], link, ROWS_BY_ROWS)
    gamma = jnp.where(flag, right_gamma, left_gamma)
    zero = jnp.zeros_like(gamma)
    gamma_turned = jnp.concatenate([zero, gamma], 1)
    inner, upper, lower, outer = wide_quarters(system_real, system_imag)
    inner = inner + 0.5 * gamma_turned
    filling = jnp.where(flag, numbers[2], numbers[1])
    gamma_padded = jnp.concatenate([gamma, zero], 1)
    source_imag = source_imag + filling * jnp.concatenate(
        [gamma_padded, jnp.zeros_like(gamma_padded)], 0
    )
    inverse = wide_inverse(inner)
    right = wide_product(inverse, upper)
    left = wide_product(lower, inverse)
    schur = outer - wide_product(left, upper)
    kept[0] = inverse
    kept[1] = right
    kept[2] = left
    kept[3] = schur
    source[:, :orbitals] = source_real
    source[:, orbitals:] = source_imag
    first, above, below, last = wide_quarters(source_real, source_imag)
    reduced = last - wide_product(left, above) - wide_product_adjoint(below, left)
    reduced = reduced + wide_product_adjoint(wide_product(left, first), left)
    corner = wide_inverse(schur)
    corner_lesser = wide_product_adjoint(wide_product(corner, reduced), corner)
    outgoing = jnp.where(flag, small, link.T)
    send[0] = sandwiched(outgoing, corner)
    send[1] = sandwiched(outgoing, corner_lesser)


def packed(real, imag):
    rows = lax.broadcasted_iota(jnp.int32, real.shape, 0)
    return jnp.where(rows > lanes_of(real), real, imag)


def complete_kernel(place, arrived, kept, source, coupling, payload):
    flag = place[0] == 1
    half = coupling.shape[0]
    orbitals = 2 * half
    incoming = jnp.where(flag, unit(half), coupling[...])
    boundary = sandwiched(incoming, arrived[0])
    boundary_lesser = sandwiched(incoming, arrived[1])
    inverse, right, left = kept[0], kept[1], kept[2]
    last = wide_inverse(kept[3] - boundary)
    lower = wide_product(last, left)
    upper = -wide_product(right, last)
    inner = inverse + wide_product(right, lower)
    top_real, top_imag = real_imag_rows(inner, upper)
    bottom_real, bottom_imag = real_imag_rows(-lower, last)
    green_real = jnp.concatenate([top_real, bottom_real], 0)
    green_imag = jnp.concatenate([top_imag, bottom_imag], 0)
    green = jnp.concatenate([green_real, green_imag], 1)
    added_real, added_imag = real_imag_rows(jnp.zeros_like(boundary_lesser), boundary_lesser)
    source_bottom = source[half:, :] + jnp.concatenate([added_real, added_imag], 1)
    sources = jnp.concatenate([source[:half, :], source_bottom], 0)
    lesser = wide_product_adjoint(wide_product(green, sources), green)
    lesser_real = flipped(flag, lesser[:, :orbitals])
    lesser_imag = flipped(flag, lesser[:, orbitals:])
    spectral_real = flipped(flag, green_real - green_real.T)
    spectral_imag = flipped(flag, green_imag + green_imag.T)
    payload[0] = packed(lesser_real, lesser_imag)
    payload[1] = packed(lesser_real + spectral_real, lesser_imag + spectral_imag)


def combine_kernel(below, above, lesser_out, greater_out):
    emitted = phonon_strength * (phonon_bose + 1.0)
    absorbed = phonon_strength * phonon_bose
    for out, mixed in (
        (lesser_out, emitted * above[0] + absorbed * below[0]),
        (greater_out, emitted * below[1] + absorbed * above[1]),
    ):
        rows = lax.broadcasted_iota(jnp.int32, mixed.shape, 0)
        lanes = lanes_of(mixed)
        mirrored = mixed.T
        out[0] = jnp.where(rows > lanes, mixed, jnp.where(rows < lanes, -mirrored, 0.0))
        out[1] = jnp.where(rows > lanes, mirrored, mixed)


def vmem(count):
    return [pl.BlockSpec(memory_space=pltpu.VMEM)] * count


def smem(count):
    return [pl.BlockSpec(memory_space=pltpu.SMEM)] * count


def on_pair(hamiltonian, coupling, contact_rates, occupation, lesser_in, greater_in, phonon_shift):
    energy_index = lax.axis_index("energy")
    energy_count = lax.axis_size("energy")
    orbitals = hamiltonian.shape[1]
    half = coupling.shape[1]
    energy_value = -1.5 + 3.0 * energy_index.astype(jnp.float32) / (energy_count - 1)
    numbers = jnp.concatenate([energy_value[None], occupation[0, 0]])
    place = lax.axis_index("dom").astype(jnp.int32)[None]
    wide = jax.ShapeDtypeStruct((4, half, orbitals), jnp.float32)
    send, kept, source = pl.pallas_call(
        eliminate_kernel,
        out_shape=(
            jax.ShapeDtypeStruct((2, half, orbitals), jnp.float32),
            wide,
            jax.ShapeDtypeStruct((orbitals, 2 * orbitals), jnp.float32),
        ),
        in_specs=smem(2) + vmem(5),
        out_specs=tuple(vmem(3)),
    )(
        place,
        numbers,
        hamiltonian[0],
        coupling[0],
        contact_rates,
        lesser_in[0, 0, 0],
        greater_in[0, 0, 0],
    )
    arrived = lax.ppermute(send, "dom", [(0, 1), (1, 0)])
    payload = pl.pallas_call(
        complete_kernel,
        out_shape=jax.ShapeDtypeStruct((2, orbitals, orbitals), jnp.float32),
        in_specs=smem(1) + vmem(4),
        out_specs=vmem(1)[0],
    )(place, arrived, kept, source, coupling[0])

    def moved(steps, value):
        count = energy_count - steps
        upward = [(start, start + steps) for start in range(count)]
        downward = [(start + steps, start) for start in range(count)]
        return (lax.ppermute(value, "energy", upward), lax.ppermute(value, "energy", downward))

    limit = min(2**QUANTUM_BITS, energy_count // 2)
    below, above = lax.switch(
        phonon_shift[0] - 1,
        [functools.partial(moved, steps) for steps in range(1, max(limit, 2))],
        payload,
    )
    block = jax.ShapeDtypeStruct((2, orbitals, orbitals), jnp.float32)
    outs = pl.pallas_call(
        combine_kernel, out_shape=(block, block), in_specs=vmem(2), out_specs=tuple(vmem(2))
    )(below, above)
    return tuple(out[None, None, None] for out in outs)


def choose(hamiltonian, coupling, contact_rates, occupation, lesser_in, greater_in, phonon_shift):
    pair = lax.axis_size("dom") == 2 and hamiltonian.shape[0] == 1 and occupation.shape[0] == 1
    lanes_fit = hamiltonian.shape[1] == 2 * coupling.shape[1] and hamiltonian.shape[1] % 128 == 0
    program = on_pair if pair and lanes_fit else on_device
    return program(
        hamiltonian, coupling, contact_rates, occupation, lesser_in, greater_in, phonon_shift
    )


def solution(mesh):
    return jax.shard_map(
        choose,
        mesh=mesh,
        in_specs=(
            P("dom", None, None),
            P("dom", None, None),
            P(),
            P(None, "energy", None),
            P(None, "energy", "dom", None, None, None),
            P(None, "energy", "dom", None, None, None),
            P(),
        ),
        out_specs=(
            P(None, "energy", "dom", None, None, None),
            P(None, "energy", "dom", None, None, None),
        ),
        check_vma=False,
    )
```

```python
import functools

import jax
import jax.numpy as jnp
from jax import lax
from jax.experimental import pallas as pl
from jax.experimental.pallas import tpu as pltpu
from jax.sharding import PartitionSpec as P

QUANTUM_BITS = 6


highest = lax.Precision.HIGHEST
broadening = 0.2
phonon_bose = 0.4
phonon_strength = 0.5


def shifted(value, axis, steps):
    count = lax.axis_size(axis)
    leading, last = (max(0, -steps), min(count, count - steps))
    return lax.ppermute(value, axis, [(source, source + steps) for source in range(leading, last)])


def from_behind(value, axis, steps):
    count = lax.axis_size(axis)
    pairs = [(source, (source + steps) % count) for source in range(count)]
    return lax.ppermute(value, axis, pairs)


def matmul_high(first_factor, second_factor):
    return jnp.matmul(first_factor, second_factor, precision=highest)


def transposed(matrix):
    return jnp.swapaxes(matrix, -1, -2)


def complex_product(first_pair, second_pair):
    return (
        matmul_high(first_pair[0], second_pair[0]) - matmul_high(first_pair[1], second_pair[1]),
        matmul_high(first_pair[0], second_pair[1]) + matmul_high(first_pair[1], second_pair[0]),
    )


def adjoint(complex_pair):
    return (transposed(complex_pair[0]), -transposed(complex_pair[1]))


def inverted(complex_pair):
    real_part, imag_part = complex_pair
    orbitals = real_part.shape[-1]
    normal_real = matmul_high(transposed(real_part), real_part) + matmul_high(
        transposed(imag_part), imag_part
    )
    normal_imag = matmul_high(transposed(real_part), imag_part) - matmul_high(
        transposed(imag_part), real_part
    )
    stacked = jnp.concatenate(
        [
            jnp.concatenate([normal_real, -normal_imag], -1),
            jnp.concatenate([normal_imag, normal_real], -1),
        ],
        -2,
    )
    factor = jnp.linalg.cholesky(stacked)
    right_side = jnp.concatenate([transposed(real_part), -transposed(imag_part)], -2)
    middle = lax.linalg.triangular_solve(factor, right_side, left_side=True, lower=True)
    solved = lax.linalg.triangular_solve(
        factor, middle, left_side=True, lower=True, transpose_a=True
    )
    return (solved[..., :orbitals, :], solved[..., orbitals:, :])


def pad_first(corner, orbitals):
    extra = orbitals - corner.shape[-1]
    return jnp.pad(corner, ((0, 0), (0, extra), (0, extra)))


def pad_last(corner, orbitals):
    extra = orbitals - corner.shape[-1]
    return jnp.pad(corner, ((0, 0), (extra, 0), (extra, 0)))


def settle(runner, stored, inbound, outbound, active):
    return lax.cond(active, lambda: runner(inbound), lambda: (stored, outbound))


def pass_right(outbound):
    return shifted(outbound, "dom", 1)


def pass_left(outbound):
    return shifted(outbound, "dom", -1)


def on_device(
    hamiltonian, coupling, contact_rates, occupation, lesser_in, greater_in, phonon_shift
):
    dom_index = lax.axis_index("dom")
    dom_count = lax.axis_size("dom")
    energy_index = lax.axis_index("energy")
    energy_count = lax.axis_size("energy")
    local_energies = occupation.shape[0]
    local_blocks = hamiltonian.shape[0]
    orbitals = hamiltonian.shape[1]
    interface = coupling.shape[1]
    total_energies = local_energies * energy_count
    global_energy = jnp.arange(local_energies, dtype=jnp.int32) * energy_count + energy_index
    energy_value = -1.5 + 3.0 * global_energy.astype(jnp.float32) / (total_energies - 1)
    identity = jnp.eye(orbitals, dtype=jnp.float32)
    extra = orbitals - interface
    gamma_left = jnp.pad(jnp.diag(contact_rates[0]), ((0, extra), (0, extra)))
    last_coupling = coupling[local_blocks - 1]
    gamma_right = jnp.pad(
        matmul_high(last_coupling * contact_rates[1][None, :], transposed(last_coupling)),
        ((extra, 0), (extra, 0)),
    )
    at_left = (dom_index == 0).astype(jnp.float32)
    at_right = (dom_index == dom_count - 1).astype(jnp.float32)

    def system(position):
        onsite = 0.5 * (hamiltonian[position] + hamiltonian[position].T)
        lesser_block = lesser_in[:, 0, position]
        greater_block = greater_in[:, 0, position]
        matrix_real = (
            energy_value[:, None, None] * identity
            - onsite
            - 0.5 * (greater_block[:, 0] - lesser_block[:, 0])
        )
        matrix_imag = broadening * identity - 0.5 * (greater_block[:, 1] - lesser_block[:, 1])
        source_imag = lesser_block[:, 1]
        matrix_imag = matrix_imag + 0.5 * at_left * gamma_left
        source_imag = source_imag + at_left * occupation[:, 0, 0, None, None] * gamma_left
        matrix_imag = matrix_imag + 0.5 * at_right * gamma_right
        source_imag = source_imag + at_right * occupation[:, 0, 1, None, None] * gamma_right
        return ((matrix_real, matrix_imag), (lesser_block[:, 0], source_imag))

    def trailing(green_block, lesser_block):
        return jnp.stack(
            [
                green_block[0][..., -interface:, -interface:],
                green_block[1][..., -interface:, -interface:],
                lesser_block[0][..., -interface:, -interface:],
                lesser_block[1][..., -interface:, -interface:],
            ]
        )

    def leading(green_block, lesser_block):
        return jnp.stack(
            [
                green_block[0][..., :interface, :interface],
                green_block[1][..., :interface, :interface],
                lesser_block[0][..., :interface, :interface],
                lesser_block[1][..., :interface, :interface],
            ]
        )

    def left_sweep(inbound):
        boundary = inbound
        matrix, source = system(0)
        matrix = (
            matrix[0] - pad_first(boundary[0], orbitals),
            matrix[1] - pad_first(boundary[1], orbitals),
        )
        source = (
            source[0] + pad_first(boundary[2], orbitals),
            source[1] + pad_first(boundary[3], orbitals),
        )
        green_block = inverted(matrix)
        lesser_block = complex_product(complex_product(green_block, source), adjoint(green_block))
        kept_blocks = [boundary]
        link_block = coupling[0]
        boundary = matmul_high(
            transposed(link_block), matmul_high(trailing(green_block, lesser_block), link_block)
        )
        return (jnp.stack(kept_blocks, 2), boundary)

    def right_sweep(inbound):
        corner = inbound
        kept_blocks = [None] * local_blocks
        for position in reversed(range(local_blocks)):
            link_block = coupling[position]
            boundary = matmul_high(link_block, matmul_high(corner, transposed(link_block)))
            matrix, source = system(position)
            matrix = (
                matrix[0] - pad_last(boundary[0], orbitals),
                matrix[1] - pad_last(boundary[1], orbitals),
            )
            source = (
                source[0] + pad_last(boundary[2], orbitals),
                source[1] + pad_last(boundary[3], orbitals),
            )
            green_block = inverted(matrix)
            lesser_block = complex_product(
                complex_product(green_block, source), adjoint(green_block)
            )
            kept_blocks[position] = boundary
            corner = leading(green_block, lesser_block)
        return (jnp.stack(kept_blocks, 2), corner)

    def ascending(section_number):
        return section_number

    def descending(section_number):
        return dom_count - 1 - section_number

    zeros_out = jnp.zeros((4, local_energies, interface, interface), jnp.float32)
    zeros_bounds = jnp.zeros((4, local_energies, local_blocks, interface, interface), jnp.float32)

    def left_runner(inbound):
        return left_sweep(inbound)

    runners = [left_runner, right_sweep]
    orderings = [ascending, descending]
    senders = [pass_right, pass_left]
    stores = [zeros_bounds, zeros_bounds]
    outbounds = [zeros_out, zeros_out]

    def advance(section_number, stores, inbounds, outbounds):
        new_stores = []
        new_outbounds = []
        for chain_number in range(len(runners)):
            active = dom_index == orderings[chain_number](section_number)
            settled = settle(
                runners[chain_number],
                stores[chain_number],
                inbounds[chain_number],
                outbounds[chain_number],
                active,
            )
            new_stores.append(settled[0])
            new_outbounds.append(settled[1])
        return (new_stores, new_outbounds)

    def turn(section_number, loop_state):
        stores, inbounds, outbounds = loop_state
        stores, outbounds = advance(section_number, stores, inbounds, outbounds)
        inbounds = [
            senders[chain_number](outbounds[chain_number]) for chain_number in range(len(runners))
        ]
        return (stores, inbounds, outbounds)

    inbounds = [jnp.zeros_like(outbound) for outbound in outbounds]
    stores, inbounds, outbounds = lax.fori_loop(
        0, dom_count - 1, turn, (stores, inbounds, outbounds)
    )
    stores, outbounds = advance(dom_count - 1, stores, inbounds, outbounds)
    left_store, right_store = stores
    position = 0
    left_part = left_store[:, :, position]
    right_part = right_store[:, :, position]
    matrix, source = system(position)
    matrix = (
        matrix[0] - pad_first(left_part[0], orbitals) - pad_last(right_part[0], orbitals),
        matrix[1] - pad_first(left_part[1], orbitals) - pad_last(right_part[1], orbitals),
    )
    source = (
        source[0] + pad_first(left_part[2], orbitals) + pad_last(right_part[2], orbitals),
        source[1] + pad_first(left_part[3], orbitals) + pad_last(right_part[3], orbitals),
    )
    green_block = inverted(matrix)
    lesser_block = complex_product(complex_product(green_block, source), adjoint(green_block))
    kept_final = [jnp.stack([green_block[0], green_block[1], lesser_block[0], lesser_block[1]])]
    final_store = jnp.stack(kept_final, 2)
    green_real = final_store[0]
    green_imag = final_store[1]
    lesser_real = final_store[2]
    lesser_imag = final_store[3]
    greater_real = lesser_real + green_real - transposed(green_real)
    greater_imag = lesser_imag + green_imag + transposed(green_imag)
    shift_amount = phonon_shift[0]
    quantum_limit = min(2**QUANTUM_BITS, total_energies // 2)
    bit_count = (quantum_limit - 1).bit_length()

    def moved_by(payload, direction):
        for bit_number in range(bit_count):
            amount = direction * 2**bit_number
            remainder = amount % energy_count
            carried = amount // energy_count
            arrived = from_behind(payload, "energy", remainder)
            aligned = jnp.where(
                energy_index < remainder,
                jnp.roll(arrived, carried + 1, axis=1),
                jnp.roll(arrived, carried, axis=1),
            )
            chosen = jnp.right_shift(shift_amount, bit_number) & 1 == 1
            payload = jnp.where(chosen, aligned, payload)
        return payload

    payload = jnp.stack([lesser_real, lesser_imag, greater_real, greater_imag])
    below = moved_by(payload, 1)
    above = moved_by(payload, -1)
    below_lesser = (below[0], below[1])
    below_greater = (below[2], below[3])
    above_lesser = (above[0], above[1])
    above_greater = (above[2], above[3])
    below_source = global_energy - shift_amount
    above_source = global_energy + shift_amount
    valid_below = ((below_source >= 0) & (below_source < total_energies)).astype(jnp.float32)[
        :, None, None, None
    ]
    valid_above = ((above_source >= 0) & (above_source < total_energies)).astype(jnp.float32)[
        :, None, None, None
    ]
    lesser_out_real = phonon_strength * (
        (phonon_bose + 1.0) * (above_lesser[0] * valid_above)
        + phonon_bose * (below_lesser[0] * valid_below)
    )
    lesser_out_imag = phonon_strength * (
        (phonon_bose + 1.0) * (above_lesser[1] * valid_above)
        + phonon_bose * (below_lesser[1] * valid_below)
    )
    greater_out_real = phonon_strength * (
        (phonon_bose + 1.0) * (below_greater[0] * valid_below)
        + phonon_bose * (above_greater[0] * valid_above)
    )
    greater_out_imag = phonon_strength * (
        (phonon_bose + 1.0) * (below_greater[1] * valid_below)
        + phonon_bose * (above_greater[1] * valid_above)
    )
    lesser_out = jnp.stack([lesser_out_real, lesser_out_imag], 2)[:, None]
    greater_out = jnp.stack([greater_out_real, greater_out_imag], 2)[:, None]
    return (lesser_out, greater_out)


MESH = pl.DeviceIdType.MESH
ROWS_BY_ROWS = (((1,), (1,)), ((), ()))
ROWS_BY_COLUMNS = (((1,), (0,)), ((), ()))


def dot(first, second, dims=ROWS_BY_COLUMNS):
    return lax.dot_general(
        first, second, dims, precision=highest, preferred_element_type=jnp.float32
    )


def lanes_of(array):
    return lax.broadcasted_iota(jnp.int32, array.shape, 1)


def times_i(wide):
    half = wide.shape[1] // 2
    moved = pltpu.roll(wide, half, 1)
    return jnp.where(lanes_of(wide) < half, -moved, moved)


def embedded(wide):
    return jnp.concatenate([wide, times_i(wide)], 0)


def wide_product(first, second):
    return dot(first, embedded(second))


def wide_product_adjoint(first, second):
    return dot(first, embedded(second), ROWS_BY_ROWS)


def twice_diagonal(matrix):
    zero = jnp.zeros_like(matrix)
    return jnp.concatenate(
        [jnp.concatenate([matrix, zero], 1), jnp.concatenate([zero, matrix], 1)], 0
    )


def sandwiched(matrix, wide):
    return dot(dot(matrix, wide), twice_diagonal(matrix), ROWS_BY_ROWS)


def scaled_row(real, imag, row):
    plain, turned = row
    return (real * plain + imag * turned, real * turned - imag * plain)


def wide_inverse(wide, group=4):
    size = wide.shape[0]
    rows = lax.broadcasted_iota(jnp.int32, wide.shape, 0)
    lanes = lanes_of(wide)
    row_lanes = lax.broadcasted_iota(jnp.int32, (1, wide.shape[1]), 1)
    for start in range(0, size, group):
        members = range(group)
        in_lanes = (lanes >= start) & (lanes < start + group)
        in_lanes = in_lanes | ((lanes >= size + start) & (lanes < size + start + group))
        in_rows = (rows >= start) & (rows < start + group)
        picked = (row_lanes >= start) & (row_lanes < start + group)
        picked = picked | ((row_lanes >= size + start) & (row_lanes < size + start + group))
        corner, held = [], []
        for member in members:
            row = wide[start + member : start + member + 1, :]
            corner.append(
                [
                    tuple(
                        jnp.broadcast_to(row[:, lane : lane + 1], row.shape)
                        for lane in (start + other, size + start + other)
                    )
                    for other in members
                ]
            )
            turned = jnp.where(picked, 0.0, times_i(row))
            row = jnp.where(picked, 0.0, row)
            row = jnp.where(row_lanes == start + member, 1.0, row)
            turned = jnp.where(row_lanes == size + start + member, 1.0, turned)
            held.append((row, turned))
        for pivot in members:
            real, imag = corner[pivot][pivot]
            scale = 1.0 / (real * real + imag * imag)
            real, imag = real * scale, -imag * scale
            held[pivot] = scaled_row(real, imag, held[pivot])
            for other in range(pivot + 1, group):
                entry = corner[pivot][other]
                corner[pivot][other] = (
                    real * entry[0] - imag * entry[1],
                    real * entry[1] + imag * entry[0],
                )
            for member in members:
                if member == pivot:
                    continue
                real, imag = corner[member][pivot]
                for other in range(pivot + 1, group):
                    entry, kept = corner[pivot][other], corner[member][other]
                    corner[member][other] = (
                        kept[0] - (real * entry[0] - imag * entry[1]),
                        kept[1] - (real * entry[1] + imag * entry[0]),
                    )
                lost = scaled_row(real, imag, held[pivot])
                held[member] = (held[member][0] - lost[0], held[member][1] - lost[1])
        updated = jnp.where(in_rows | in_lanes, 0.0, wide)
        for member in members:
            lane = start + member
            column_real = jnp.broadcast_to(wide[:, lane : lane + 1], wide.shape)
            lane = size + lane
            column_imag = jnp.broadcast_to(wide[:, lane : lane + 1], wide.shape)
            at_member = (rows == start + member).astype(jnp.float32)
            column_real = jnp.where(in_rows, -at_member, column_real)
            column_imag = jnp.where(in_rows, 0.0, column_imag)
            updated = updated - column_real * held[member][0] - column_imag * held[member][1]
        wide = updated
    return wide


def flipped(flag, matrix):
    half = matrix.shape[0] // 2
    moved = pltpu.roll(matrix, half, 1)
    moved = jnp.concatenate([moved[half:], moved[:half]], 0)
    return jnp.where(flag, moved, matrix)


def wide_quarters(real, imag):
    half = real.shape[0] // 2
    left_lanes = lax.broadcasted_iota(jnp.int32, (half, 2 * half), 1) < half
    quarters = []
    for start in (0, half):
        real_rows, imag_rows = real[start : start + half], imag[start : start + half]
        quarters.append(jnp.where(left_lanes, real_rows, pltpu.roll(imag_rows, half, 1)))
        quarters.append(jnp.where(left_lanes, pltpu.roll(real_rows, half, 1), imag_rows))
    return quarters


def real_imag_rows(left, right):
    half = left.shape[0]
    left_lanes = lanes_of(left) < half
    return (
        jnp.where(left_lanes, left, pltpu.roll(right, half, 1)),
        jnp.where(left_lanes, pltpu.roll(left, half, 1), right),
    )


def unit(size):
    rows = lax.broadcasted_iota(jnp.int32, (size, size), 0)
    return (rows == lax.broadcasted_iota(jnp.int32, (size, size), 1)).astype(jnp.float32)


def packed(real, imag):
    rows = lax.broadcasted_iota(jnp.int32, real.shape, 0)
    return jnp.where(rows > lanes_of(real), real, imag)


def pair_kernel(
    numbers,
    hamiltonian,
    coupling,
    rates,
    lesser,
    greater,
    payload,
    outgoing_corners,
    arrived,
    send_sems,
    recv_sems,
):
    place = lax.axis_index("dom")
    partner = 1 - place
    barrier = pltpu.get_barrier_semaphore()
    pl.semaphore_signal(barrier, inc=1, device_id={"dom": partner}, device_id_type=MESH)
    flag = place == 1
    orbitals = hamiltonian.shape[0]
    half = coupling.shape[0]
    identity = unit(orbitals)
    link = coupling[...]
    system_real = (
        numbers[0] * identity
        - 0.5 * (hamiltonian[...] + hamiltonian[...].T)
        - 0.5 * (greater[0] - lesser[0])
    )
    system_imag = broadening * identity - 0.5 * (greater[1] - lesser[1])
    system_real = flipped(flag, system_real)
    system_imag = flipped(flag, system_imag)
    source_real = flipped(flag, lesser[0])
    source_imag = flipped(flag, lesser[1])
    small = unit(half)
    left_gamma = small * rates[0:1, :]
    right_gamma = dot(link * rates[1:2, :], link, ROWS_BY_ROWS)
    gamma = jnp.where(flag, right_gamma, left_gamma)
    zero = jnp.zeros_like(gamma)
    gamma_turned = jnp.concatenate([zero, gamma], 1)
    inner, upper, lower, outer = wide_quarters(system_real, system_imag)
    inner = inner + 0.5 * gamma_turned
    filling = jnp.where(flag, numbers[2], numbers[1])
    gamma_padded = jnp.concatenate([gamma, zero], 1)
    source_imag = source_imag + filling * jnp.concatenate(
        [gamma_padded, jnp.zeros_like(gamma_padded)], 0
    )
    inverse = wide_inverse(inner)
    right = wide_product(inverse, upper)
    left = wide_product(lower, inverse)
    schur = outer - wide_product(left, upper)
    outgoing = jnp.where(flag, small, link.T)
    copies = [
        pltpu.make_async_remote_copy(
            src_ref=outgoing_corners.at[part],
            dst_ref=arrived.at[part],
            send_sem=send_sems.at[part],
            recv_sem=recv_sems.at[part],
            device_id={"dom": partner},
            device_id_type=MESH,
        )
        for part in range(2)
    ]
    first, above, below, last = wide_quarters(source_real, source_imag)
    reduced = last - wide_product(left, above) - wide_product_adjoint(below, left)
    reduced = reduced + wide_product_adjoint(wide_product(left, first), left)
    corner = wide_inverse(schur)
    outgoing_corners[0] = sandwiched(outgoing, corner)
    pl.semaphore_wait(barrier, 1)
    copies[0].start()
    corner_lesser = wide_product_adjoint(wide_product(corner, reduced), corner)
    outgoing_corners[1] = sandwiched(outgoing, corner_lesser)
    copies[1].start()
    incoming = jnp.where(flag, small, link)
    copies[0].wait()
    last = wide_inverse(schur - sandwiched(incoming, arrived[0]))
    lower = wide_product(last, left)
    upper = -wide_product(right, last)
    inner = inverse + wide_product(right, lower)
    top_real, top_imag = real_imag_rows(inner, upper)
    bottom_real, bottom_imag = real_imag_rows(-lower, last)
    green_real = jnp.concatenate([top_real, bottom_real], 0)
    green_imag = jnp.concatenate([top_imag, bottom_imag], 0)
    green = jnp.concatenate([green_real, green_imag], 1)
    copies[1].wait()
    boundary_lesser = sandwiched(incoming, arrived[1])
    added_real, added_imag = real_imag_rows(jnp.zeros_like(boundary_lesser), boundary_lesser)
    source = jnp.concatenate([source_real, source_imag], 1)
    source_bottom = source[half:, :] + jnp.concatenate([added_real, added_imag], 1)
    sources = jnp.concatenate([source[:half, :], source_bottom], 0)
    lesser = wide_product_adjoint(wide_product(green, sources), green)
    lesser_real = flipped(flag, lesser[:, :orbitals])
    lesser_imag = flipped(flag, lesser[:, orbitals:])
    spectral_real = flipped(flag, green_real - green_real.T)
    spectral_imag = flipped(flag, green_imag + green_imag.T)
    payload[0] = packed(lesser_real, lesser_imag)
    payload[1] = packed(lesser_real + spectral_real, lesser_imag + spectral_imag)


def shift_kernel(steps, payload, mixed, below, above, send_sems, recv_sems):
    here = lax.axis_index("energy")
    count = lax.axis_size("energy")
    has_below, has_above = here >= steps, here + steps < count
    lower, higher = jnp.maximum(here - steps, 0), jnp.minimum(here + steps, count - 1)
    barrier = pltpu.get_barrier_semaphore()

    def copy(part, direction):
        slot = 2 * part + direction
        return pltpu.make_async_remote_copy(
            src_ref=payload.at[part],
            dst_ref=(below, above)[direction].at[part],
            send_sem=send_sems.at[slot],
            recv_sem=recv_sems.at[slot],
            device_id={"energy": (higher, lower)[direction]},
            device_id_type=MESH,
        )

    @pl.when(has_below)
    def _():
        pl.semaphore_signal(barrier, inc=1, device_id={"energy": lower}, device_id_type=MESH)

    @pl.when(has_above)
    def _():
        pl.semaphore_signal(barrier, inc=1, device_id={"energy": higher}, device_id_type=MESH)

    @pl.when(jnp.logical_not(has_below))
    def _():
        below[...] = jnp.zeros_like(below)

    @pl.when(jnp.logical_not(has_above))
    def _():
        above[...] = jnp.zeros_like(above)

    pl.semaphore_wait(barrier, has_below.astype(jnp.int32) + has_above.astype(jnp.int32))

    for part in range(2):
        for direction, sends in ((0, has_above), (1, has_below)):
            pl.when(sends)(functools.partial(lambda *at: copy(*at).start(), part, direction))
    emitted = phonon_strength * (phonon_bose + 1.0)
    absorbed = phonon_strength * phonon_bose
    for part, (from_below, from_above) in enumerate(((absorbed, emitted), (emitted, absorbed))):
        for direction, receives in ((0, has_below), (1, has_above)):
            pl.when(receives)(functools.partial(lambda *at: copy(*at).wait_recv(), part, direction))
        mixed[part] = from_below * below[part] + from_above * above[part]
    for part in range(2):
        for direction, sends in ((0, has_above), (1, has_below)):
            pl.when(sends)(functools.partial(lambda *at: copy(*at).wait_send(), part, direction))


def unpack_kernel(mixed, lesser_out, greater_out):
    for part, out in enumerate((lesser_out, greater_out)):
        held = mixed[part]
        rows = lax.broadcasted_iota(jnp.int32, held.shape, 0)
        lanes = lanes_of(held)
        mirrored = held.T
        out[0] = jnp.where(rows > lanes, held, jnp.where(rows < lanes, -mirrored, 0.0))
        out[1] = jnp.where(rows > lanes, mirrored, held)


def vmem(count):
    return [pl.BlockSpec(memory_space=pltpu.VMEM)] * count


def smem(count):
    return [pl.BlockSpec(memory_space=pltpu.SMEM)] * count


def on_pair(hamiltonian, coupling, contact_rates, occupation, lesser_in, greater_in, phonon_shift):
    energy_index = lax.axis_index("energy")
    energy_count = lax.axis_size("energy")
    orbitals = hamiltonian.shape[1]
    half = coupling.shape[1]
    energy_value = -1.5 + 3.0 * energy_index.astype(jnp.float32) / (energy_count - 1)
    numbers = jnp.concatenate([energy_value[None], occupation[0, 0]])
    packed_pair = jax.ShapeDtypeStruct((2, orbitals, orbitals), jnp.float32)
    corners = pltpu.VMEM((2, half, orbitals), jnp.float32)
    payload = pl.pallas_call(
        pair_kernel,
        out_shape=packed_pair,
        in_specs=smem(1) + vmem(5),
        out_specs=vmem(1)[0],
        scratch_shapes=[corners, corners] + [pltpu.SemaphoreType.DMA((2,))] * 2,
        compiler_params=pltpu.CompilerParams(collective_id=0, has_side_effects=True),
    )(
        numbers,
        hamiltonian[0],
        coupling[0],
        contact_rates,
        lesser_in[0, 0, 0],
        greater_in[0, 0, 0],
    )

    def moved(steps, value):
        landing = pltpu.VMEM((2, orbitals, orbitals), jnp.float32)
        return pl.pallas_call(
            functools.partial(shift_kernel, steps),
            out_shape=packed_pair,
            in_specs=vmem(1),
            out_specs=vmem(1)[0],
            scratch_shapes=[landing, landing] + [pltpu.SemaphoreType.DMA((4,))] * 2,
            compiler_params=pltpu.CompilerParams(collective_id=steps, has_side_effects=True),
        )(value)

    limit = min(2**QUANTUM_BITS, energy_count // 2)
    mixed = lax.switch(
        phonon_shift[0] - 1,
        [functools.partial(moved, steps) for steps in range(1, max(limit, 2))],
        payload,
    )
    outs = pl.pallas_call(
        unpack_kernel,
        out_shape=(packed_pair, packed_pair),
        in_specs=vmem(1),
        out_specs=tuple(vmem(2)),
    )(mixed)
    return tuple(out[None, None, None] for out in outs)


def choose(hamiltonian, coupling, contact_rates, occupation, lesser_in, greater_in, phonon_shift):
    pair = lax.axis_size("dom") == 2 and hamiltonian.shape[0] == 1 and occupation.shape[0] == 1
    lanes_fit = hamiltonian.shape[1] == 2 * coupling.shape[1] and hamiltonian.shape[1] % 128 == 0
    program = on_pair if pair and lanes_fit else on_device
    return program(
        hamiltonian, coupling, contact_rates, occupation, lesser_in, greater_in, phonon_shift
    )


def solution(mesh):
    return jax.shard_map(
        choose,
        mesh=mesh,
        in_specs=(
            P("dom", None, None),
            P("dom", None, None),
            P(),
            P(None, "energy", None),
            P(None, "energy", "dom", None, None, None),
            P(None, "energy", "dom", None, None, None),
            P(),
        ),
        out_specs=(
            P(None, "energy", "dom", None, None, None),
            P(None, "energy", "dom", None, None, None),
        ),
        check_vma=False,
    )
```

```python
import functools

import jax
import jax.numpy as jnp
from jax import lax
from jax.experimental import pallas as pl
from jax.experimental.pallas import tpu as pltpu
from jax.sharding import PartitionSpec as P

QUANTUM_BITS = 6


highest = lax.Precision.HIGHEST
broadening = 0.2
phonon_bose = 0.4
phonon_strength = 0.5


def shifted(value, axis, steps):
    count = lax.axis_size(axis)
    leading, last = (max(0, -steps), min(count, count - steps))
    return lax.ppermute(value, axis, [(source, source + steps) for source in range(leading, last)])


def from_behind(value, axis, steps):
    count = lax.axis_size(axis)
    pairs = [(source, (source + steps) % count) for source in range(count)]
    return lax.ppermute(value, axis, pairs)


def matmul_high(first_factor, second_factor):
    return jnp.matmul(first_factor, second_factor, precision=highest)


def transposed(matrix):
    return jnp.swapaxes(matrix, -1, -2)


def complex_product(first_pair, second_pair):
    return (
        matmul_high(first_pair[0], second_pair[0]) - matmul_high(first_pair[1], second_pair[1]),
        matmul_high(first_pair[0], second_pair[1]) + matmul_high(first_pair[1], second_pair[0]),
    )


def adjoint(complex_pair):
    return (transposed(complex_pair[0]), -transposed(complex_pair[1]))


def inverted(complex_pair):
    real_part, imag_part = complex_pair
    orbitals = real_part.shape[-1]
    normal_real = matmul_high(transposed(real_part), real_part) + matmul_high(
        transposed(imag_part), imag_part
    )
    normal_imag = matmul_high(transposed(real_part), imag_part) - matmul_high(
        transposed(imag_part), real_part
    )
    stacked = jnp.concatenate(
        [
            jnp.concatenate([normal_real, -normal_imag], -1),
            jnp.concatenate([normal_imag, normal_real], -1),
        ],
        -2,
    )
    factor = jnp.linalg.cholesky(stacked)
    right_side = jnp.concatenate([transposed(real_part), -transposed(imag_part)], -2)
    middle = lax.linalg.triangular_solve(factor, right_side, left_side=True, lower=True)
    solved = lax.linalg.triangular_solve(
        factor, middle, left_side=True, lower=True, transpose_a=True
    )
    return (solved[..., :orbitals, :], solved[..., orbitals:, :])


def pad_first(corner, orbitals):
    extra = orbitals - corner.shape[-1]
    return jnp.pad(corner, ((0, 0), (0, extra), (0, extra)))


def pad_last(corner, orbitals):
    extra = orbitals - corner.shape[-1]
    return jnp.pad(corner, ((0, 0), (extra, 0), (extra, 0)))


def settle(runner, stored, inbound, outbound, active):
    return lax.cond(active, lambda: runner(inbound), lambda: (stored, outbound))


def pass_right(outbound):
    return shifted(outbound, "dom", 1)


def pass_left(outbound):
    return shifted(outbound, "dom", -1)


def on_device(
    hamiltonian, coupling, contact_rates, occupation, lesser_in, greater_in, phonon_shift
):
    dom_index = lax.axis_index("dom")
    dom_count = lax.axis_size("dom")
    energy_index = lax.axis_index("energy")
    energy_count = lax.axis_size("energy")
    local_energies = occupation.shape[0]
    local_blocks = hamiltonian.shape[0]
    orbitals = hamiltonian.shape[1]
    interface = coupling.shape[1]
    total_energies = local_energies * energy_count
    global_energy = jnp.arange(local_energies, dtype=jnp.int32) * energy_count + energy_index
    energy_value = -1.5 + 3.0 * global_energy.astype(jnp.float32) / (total_energies - 1)
    identity = jnp.eye(orbitals, dtype=jnp.float32)
    extra = orbitals - interface
    gamma_left = jnp.pad(jnp.diag(contact_rates[0]), ((0, extra), (0, extra)))
    last_coupling = coupling[local_blocks - 1]
    gamma_right = jnp.pad(
        matmul_high(last_coupling * contact_rates[1][None, :], transposed(last_coupling)),
        ((extra, 0), (extra, 0)),
    )
    at_left = (dom_index == 0).astype(jnp.float32)
    at_right = (dom_index == dom_count - 1).astype(jnp.float32)

    def system(position):
        onsite = 0.5 * (hamiltonian[position] + hamiltonian[position].T)
        lesser_block = lesser_in[:, 0, position]
        greater_block = greater_in[:, 0, position]
        matrix_real = (
            energy_value[:, None, None] * identity
            - onsite
            - 0.5 * (greater_block[:, 0] - lesser_block[:, 0])
        )
        matrix_imag = broadening * identity - 0.5 * (greater_block[:, 1] - lesser_block[:, 1])
        source_imag = lesser_block[:, 1]
        matrix_imag = matrix_imag + 0.5 * at_left * gamma_left
        source_imag = source_imag + at_left * occupation[:, 0, 0, None, None] * gamma_left
        matrix_imag = matrix_imag + 0.5 * at_right * gamma_right
        source_imag = source_imag + at_right * occupation[:, 0, 1, None, None] * gamma_right
        return ((matrix_real, matrix_imag), (lesser_block[:, 0], source_imag))

    def trailing(green_block, lesser_block):
        return jnp.stack(
            [
                green_block[0][..., -interface:, -interface:],
                green_block[1][..., -interface:, -interface:],
                lesser_block[0][..., -interface:, -interface:],
                lesser_block[1][..., -interface:, -interface:],
            ]
        )

    def leading(green_block, lesser_block):
        return jnp.stack(
            [
                green_block[0][..., :interface, :interface],
                green_block[1][..., :interface, :interface],
                lesser_block[0][..., :interface, :interface],
                lesser_block[1][..., :interface, :interface],
            ]
        )

    def left_sweep(inbound):
        boundary = inbound
        matrix, source = system(0)
        matrix = (
            matrix[0] - pad_first(boundary[0], orbitals),
            matrix[1] - pad_first(boundary[1], orbitals),
        )
        source = (
            source[0] + pad_first(boundary[2], orbitals),
            source[1] + pad_first(boundary[3], orbitals),
        )
        green_block = inverted(matrix)
        lesser_block = complex_product(complex_product(green_block, source), adjoint(green_block))
        kept_blocks = [boundary]
        link_block = coupling[0]
        boundary = matmul_high(
            transposed(link_block), matmul_high(trailing(green_block, lesser_block), link_block)
        )
        return (jnp.stack(kept_blocks, 2), boundary)

    def right_sweep(inbound):
        corner = inbound
        kept_blocks = [None] * local_blocks
        for position in reversed(range(local_blocks)):
            link_block = coupling[position]
            boundary = matmul_high(link_block, matmul_high(corner, transposed(link_block)))
            matrix, source = system(position)
            matrix = (
                matrix[0] - pad_last(boundary[0], orbitals),
                matrix[1] - pad_last(boundary[1], orbitals),
            )
            source = (
                source[0] + pad_last(boundary[2], orbitals),
                source[1] + pad_last(boundary[3], orbitals),
            )
            green_block = inverted(matrix)
            lesser_block = complex_product(
                complex_product(green_block, source), adjoint(green_block)
            )
            kept_blocks[position] = boundary
            corner = leading(green_block, lesser_block)
        return (jnp.stack(kept_blocks, 2), corner)

    def ascending(section_number):
        return section_number

    def descending(section_number):
        return dom_count - 1 - section_number

    zeros_out = jnp.zeros((4, local_energies, interface, interface), jnp.float32)
    zeros_bounds = jnp.zeros((4, local_energies, local_blocks, interface, interface), jnp.float32)

    def left_runner(inbound):
        return left_sweep(inbound)

    runners = [left_runner, right_sweep]
    orderings = [ascending, descending]
    senders = [pass_right, pass_left]
    stores = [zeros_bounds, zeros_bounds]
    outbounds = [zeros_out, zeros_out]

    def advance(section_number, stores, inbounds, outbounds):
        new_stores = []
        new_outbounds = []
        for chain_number in range(len(runners)):
            active = dom_index == orderings[chain_number](section_number)
            settled = settle(
                runners[chain_number],
                stores[chain_number],
                inbounds[chain_number],
                outbounds[chain_number],
                active,
            )
            new_stores.append(settled[0])
            new_outbounds.append(settled[1])
        return (new_stores, new_outbounds)

    def turn(section_number, loop_state):
        stores, inbounds, outbounds = loop_state
        stores, outbounds = advance(section_number, stores, inbounds, outbounds)
        inbounds = [
            senders[chain_number](outbounds[chain_number]) for chain_number in range(len(runners))
        ]
        return (stores, inbounds, outbounds)

    inbounds = [jnp.zeros_like(outbound) for outbound in outbounds]
    stores, inbounds, outbounds = lax.fori_loop(
        0, dom_count - 1, turn, (stores, inbounds, outbounds)
    )
    stores, outbounds = advance(dom_count - 1, stores, inbounds, outbounds)
    left_store, right_store = stores
    position = 0
    left_part = left_store[:, :, position]
    right_part = right_store[:, :, position]
    matrix, source = system(position)
    matrix = (
        matrix[0] - pad_first(left_part[0], orbitals) - pad_last(right_part[0], orbitals),
        matrix[1] - pad_first(left_part[1], orbitals) - pad_last(right_part[1], orbitals),
    )
    source = (
        source[0] + pad_first(left_part[2], orbitals) + pad_last(right_part[2], orbitals),
        source[1] + pad_first(left_part[3], orbitals) + pad_last(right_part[3], orbitals),
    )
    green_block = inverted(matrix)
    lesser_block = complex_product(complex_product(green_block, source), adjoint(green_block))
    kept_final = [jnp.stack([green_block[0], green_block[1], lesser_block[0], lesser_block[1]])]
    final_store = jnp.stack(kept_final, 2)
    green_real = final_store[0]
    green_imag = final_store[1]
    lesser_real = final_store[2]
    lesser_imag = final_store[3]
    greater_real = lesser_real + green_real - transposed(green_real)
    greater_imag = lesser_imag + green_imag + transposed(green_imag)
    shift_amount = phonon_shift[0]
    quantum_limit = min(2**QUANTUM_BITS, total_energies // 2)
    bit_count = (quantum_limit - 1).bit_length()

    def moved_by(payload, direction):
        for bit_number in range(bit_count):
            amount = direction * 2**bit_number
            remainder = amount % energy_count
            carried = amount // energy_count
            arrived = from_behind(payload, "energy", remainder)
            aligned = jnp.where(
                energy_index < remainder,
                jnp.roll(arrived, carried + 1, axis=1),
                jnp.roll(arrived, carried, axis=1),
            )
            chosen = jnp.right_shift(shift_amount, bit_number) & 1 == 1
            payload = jnp.where(chosen, aligned, payload)
        return payload

    payload = jnp.stack([lesser_real, lesser_imag, greater_real, greater_imag])
    below = moved_by(payload, 1)
    above = moved_by(payload, -1)
    below_lesser = (below[0], below[1])
    below_greater = (below[2], below[3])
    above_lesser = (above[0], above[1])
    above_greater = (above[2], above[3])
    below_source = global_energy - shift_amount
    above_source = global_energy + shift_amount
    valid_below = ((below_source >= 0) & (below_source < total_energies)).astype(jnp.float32)[
        :, None, None, None
    ]
    valid_above = ((above_source >= 0) & (above_source < total_energies)).astype(jnp.float32)[
        :, None, None, None
    ]
    lesser_out_real = phonon_strength * (
        (phonon_bose + 1.0) * (above_lesser[0] * valid_above)
        + phonon_bose * (below_lesser[0] * valid_below)
    )
    lesser_out_imag = phonon_strength * (
        (phonon_bose + 1.0) * (above_lesser[1] * valid_above)
        + phonon_bose * (below_lesser[1] * valid_below)
    )
    greater_out_real = phonon_strength * (
        (phonon_bose + 1.0) * (below_greater[0] * valid_below)
        + phonon_bose * (above_greater[0] * valid_above)
    )
    greater_out_imag = phonon_strength * (
        (phonon_bose + 1.0) * (below_greater[1] * valid_below)
        + phonon_bose * (above_greater[1] * valid_above)
    )
    lesser_out = jnp.stack([lesser_out_real, lesser_out_imag], 2)[:, None]
    greater_out = jnp.stack([greater_out_real, greater_out_imag], 2)[:, None]
    return (lesser_out, greater_out)


MESH = pl.DeviceIdType.MESH
ROWS_BY_ROWS = (((1,), (1,)), ((), ()))
ROWS_BY_COLUMNS = (((1,), (0,)), ((), ()))


def dot(first, second, dims=ROWS_BY_COLUMNS):
    return lax.dot_general(
        first, second, dims, precision=highest, preferred_element_type=jnp.float32
    )


def lanes_of(array):
    return lax.broadcasted_iota(jnp.int32, array.shape, 1)


def times_i(wide):
    half = wide.shape[1] // 2
    moved = pltpu.roll(wide, half, 1)
    return jnp.where(lanes_of(wide) < half, -moved, moved)


def embedded(wide):
    return jnp.concatenate([wide, times_i(wide)], 0)


def wide_product(first, second):
    return dot(first, embedded(second))


def wide_product_adjoint(first, second):
    return dot(first, embedded(second), ROWS_BY_ROWS)


def twice_diagonal(matrix):
    zero = jnp.zeros_like(matrix)
    return jnp.concatenate(
        [jnp.concatenate([matrix, zero], 1), jnp.concatenate([zero, matrix], 1)], 0
    )


def sandwiched(matrix, wide):
    return dot(dot(matrix, wide), twice_diagonal(matrix), ROWS_BY_ROWS)


def scaled_row(real, imag, row):
    plain, turned = row
    return (real * plain + imag * turned, real * turned - imag * plain)


def wide_inverse(wide, group=4):
    size = wide.shape[0]
    rows = lax.broadcasted_iota(jnp.int32, wide.shape, 0)
    lanes = lanes_of(wide)
    row_lanes = lax.broadcasted_iota(jnp.int32, (1, wide.shape[1]), 1)
    for start in range(0, size, group):
        members = range(group)
        in_lanes = (lanes >= start) & (lanes < start + group)
        in_lanes = in_lanes | ((lanes >= size + start) & (lanes < size + start + group))
        in_rows = (rows >= start) & (rows < start + group)
        picked = (row_lanes >= start) & (row_lanes < start + group)
        picked = picked | ((row_lanes >= size + start) & (row_lanes < size + start + group))
        corner, held = [], []
        for member in members:
            row = wide[start + member : start + member + 1, :]
            corner.append(
                [
                    tuple(
                        jnp.broadcast_to(row[:, lane : lane + 1], row.shape)
                        for lane in (start + other, size + start + other)
                    )
                    for other in members
                ]
            )
            turned = jnp.where(picked, 0.0, times_i(row))
            row = jnp.where(picked, 0.0, row)
            row = jnp.where(row_lanes == start + member, 1.0, row)
            turned = jnp.where(row_lanes == size + start + member, 1.0, turned)
            held.append((row, turned))
        for pivot in members:
            real, imag = corner[pivot][pivot]
            scale = 1.0 / (real * real + imag * imag)
            real, imag = real * scale, -imag * scale
            held[pivot] = scaled_row(real, imag, held[pivot])
            for other in range(pivot + 1, group):
                entry = corner[pivot][other]
                corner[pivot][other] = (
                    real * entry[0] - imag * entry[1],
                    real * entry[1] + imag * entry[0],
                )
            for member in members:
                if member == pivot:
                    continue
                real, imag = corner[member][pivot]
                for other in range(pivot + 1, group):
                    entry, kept = corner[pivot][other], corner[member][other]
                    corner[member][other] = (
                        kept[0] - (real * entry[0] - imag * entry[1]),
                        kept[1] - (real * entry[1] + imag * entry[0]),
                    )
                lost = scaled_row(real, imag, held[pivot])
                held[member] = (held[member][0] - lost[0], held[member][1] - lost[1])
        updated = jnp.where(in_rows | in_lanes, 0.0, wide)
        for member in members:
            lane = start + member
            column_real = jnp.broadcast_to(wide[:, lane : lane + 1], wide.shape)
            lane = size + lane
            column_imag = jnp.broadcast_to(wide[:, lane : lane + 1], wide.shape)
            at_member = (rows == start + member).astype(jnp.float32)
            column_real = jnp.where(in_rows, -at_member, column_real)
            column_imag = jnp.where(in_rows, 0.0, column_imag)
            updated = updated - column_real * held[member][0] - column_imag * held[member][1]
        wide = updated
    return wide


def flipped(flag, matrix):
    half = matrix.shape[0] // 2
    moved = pltpu.roll(matrix, half, 1)
    moved = jnp.concatenate([moved[half:], moved[:half]], 0)
    return jnp.where(flag, moved, matrix)


def wide_quarters(real, imag):
    half = real.shape[0] // 2
    left_lanes = lax.broadcasted_iota(jnp.int32, (half, 2 * half), 1) < half
    quarters = []
    for start in (0, half):
        real_rows, imag_rows = real[start : start + half], imag[start : start + half]
        quarters.append(jnp.where(left_lanes, real_rows, pltpu.roll(imag_rows, half, 1)))
        quarters.append(jnp.where(left_lanes, pltpu.roll(real_rows, half, 1), imag_rows))
    return quarters


def real_imag_rows(left, right):
    half = left.shape[0]
    left_lanes = lanes_of(left) < half
    return (
        jnp.where(left_lanes, left, pltpu.roll(right, half, 1)),
        jnp.where(left_lanes, pltpu.roll(left, half, 1), right),
    )


def unit(size):
    rows = lax.broadcasted_iota(jnp.int32, (size, size), 0)
    return (rows == lax.broadcasted_iota(jnp.int32, (size, size), 1)).astype(jnp.float32)


def packed(real, imag):
    rows = lax.broadcasted_iota(jnp.int32, real.shape, 0)
    return jnp.where(rows > lanes_of(real), real, imag)


def pair_kernel(
    occupation,
    hamiltonian,
    coupling,
    rates,
    lesser,
    greater,
    payload,
    outgoing_corners,
    arrived,
    arrived_link,
    send_sems,
    recv_sems,
):
    place = lax.axis_index("dom")
    partner = 1 - place
    barrier = pltpu.get_barrier_semaphore()
    pl.semaphore_signal(barrier, inc=1, device_id={"dom": partner}, device_id_type=MESH)
    flag = place == 1
    energy_index = lax.axis_index("energy").astype(jnp.float32)
    energy_value = -1.5 + 3.0 * energy_index / (lax.axis_size("energy") - 1)
    orbitals = hamiltonian.shape[0]
    half = coupling.shape[0]
    identity = unit(orbitals)
    link = coupling[...]
    system_real = (
        energy_value * identity
        - 0.5 * (hamiltonian[...] + hamiltonian[...].T)
        - 0.5 * (greater[0] - lesser[0])
    )
    system_imag = broadening * identity - 0.5 * (greater[1] - lesser[1])
    system_real = flipped(flag, system_real)
    system_imag = flipped(flag, system_imag)
    source_real = flipped(flag, lesser[0])
    source_imag = flipped(flag, lesser[1])
    small = unit(half)
    left_gamma = small * rates[0:1, :]
    right_gamma = dot(link * rates[1:2, :], link, ROWS_BY_ROWS)
    gamma = jnp.where(flag, right_gamma, left_gamma)
    zero = jnp.zeros_like(gamma)
    gamma_turned = jnp.concatenate([zero, gamma], 1)
    inner, upper, lower, outer = wide_quarters(system_real, system_imag)
    inner = inner + 0.5 * gamma_turned
    filling = jnp.where(flag, occupation[:, 1:2], occupation[:, 0:1])
    gamma_padded = jnp.concatenate([gamma, zero], 1)
    source_imag = source_imag + filling * jnp.concatenate(
        [gamma_padded, jnp.zeros_like(gamma_padded)], 0
    )
    inverse = wide_inverse(inner)
    copies = [
        pltpu.make_async_remote_copy(
            src_ref=origin,
            dst_ref=target,
            send_sem=send_sems.at[part],
            recv_sem=recv_sems.at[part],
            device_id={"dom": partner},
            device_id_type=MESH,
        )
        for part, (origin, target) in enumerate(
            (
                (outgoing_corners.at[0], arrived.at[0]),
                (outgoing_corners.at[1], arrived.at[1]),
                (coupling, arrived_link),
            )
        )
    ]
    pl.semaphore_wait(barrier, 1)
    copies[2].start()
    right = wide_product(inverse, upper)
    left = wide_product(lower, inverse)
    schur = outer - wide_product(left, upper)
    first, above, below, last = wide_quarters(source_real, source_imag)
    reduced = last - wide_product(left, above) - wide_product_adjoint(below, left)
    reduced = reduced + wide_product_adjoint(wide_product(left, first), left)
    corner = wide_inverse(schur)
    outgoing_corners[0] = corner
    copies[0].start()
    corner_lesser = wide_product_adjoint(wide_product(corner, reduced), corner)
    outgoing_corners[1] = corner_lesser
    copies[1].start()
    copies[2].wait()
    incoming = jnp.where(flag, arrived_link[...].T, link)
    copies[0].wait()
    last = wide_inverse(schur - sandwiched(incoming, arrived[0]))
    lower = wide_product(last, left)
    upper = -wide_product(right, last)
    inner = inverse + wide_product(right, lower)
    top_real, top_imag = real_imag_rows(inner, upper)
    bottom_real, bottom_imag = real_imag_rows(-lower, last)
    green_real = jnp.concatenate([top_real, bottom_real], 0)
    green_imag = jnp.concatenate([top_imag, bottom_imag], 0)
    green = jnp.concatenate([green_real, green_imag], 1)
    copies[1].wait()
    boundary_lesser = sandwiched(incoming, arrived[1])
    added_real, added_imag = real_imag_rows(jnp.zeros_like(boundary_lesser), boundary_lesser)
    source = jnp.concatenate([source_real, source_imag], 1)
    source_bottom = source[half:, :] + jnp.concatenate([added_real, added_imag], 1)
    sources = jnp.concatenate([source[:half, :], source_bottom], 0)
    lesser = wide_product_adjoint(wide_product(green, sources), green)
    lesser_real = flipped(flag, lesser[:, :orbitals])
    lesser_imag = flipped(flag, lesser[:, orbitals:])
    spectral_real = flipped(flag, green_real - green_real.T)
    spectral_imag = flipped(flag, green_imag + green_imag.T)
    payload[0] = packed(lesser_real, lesser_imag)
    payload[1] = packed(lesser_real + spectral_real, lesser_imag + spectral_imag)


def shift_kernel(steps, payload, mixed, below, above, send_sems, recv_sems):
    here = lax.axis_index("energy")
    count = lax.axis_size("energy")
    has_below, has_above = here >= steps, here + steps < count
    lower, higher = jnp.maximum(here - steps, 0), jnp.minimum(here + steps, count - 1)
    barrier = pltpu.get_barrier_semaphore()

    def copy(part, direction):
        slot = 2 * part + direction
        return pltpu.make_async_remote_copy(
            src_ref=payload.at[part],
            dst_ref=(below, above)[direction].at[part],
            send_sem=send_sems.at[slot],
            recv_sem=recv_sems.at[slot],
            device_id={"energy": (higher, lower)[direction]},
            device_id_type=MESH,
        )

    @pl.when(has_below)
    def _():
        pl.semaphore_signal(barrier, inc=1, device_id={"energy": lower}, device_id_type=MESH)

    @pl.when(has_above)
    def _():
        pl.semaphore_signal(barrier, inc=1, device_id={"energy": higher}, device_id_type=MESH)

    @pl.when(jnp.logical_not(has_below))
    def _():
        below[...] = jnp.zeros_like(below)

    @pl.when(jnp.logical_not(has_above))
    def _():
        above[...] = jnp.zeros_like(above)

    pl.semaphore_wait(barrier, has_below.astype(jnp.int32) + has_above.astype(jnp.int32))

    for part in range(2):
        for direction, sends in ((0, has_above), (1, has_below)):
            pl.when(sends)(functools.partial(lambda *at: copy(*at).start(), part, direction))
    emitted = phonon_strength * (phonon_bose + 1.0)
    absorbed = phonon_strength * phonon_bose
    for part, (from_below, from_above) in enumerate(((absorbed, emitted), (emitted, absorbed))):
        for direction, receives in ((0, has_below), (1, has_above)):
            pl.when(receives)(functools.partial(lambda *at: copy(*at).wait_recv(), part, direction))
        mixed[part] = from_below * below[part] + from_above * above[part]
    for part in range(2):
        for direction, sends in ((0, has_above), (1, has_below)):
            pl.when(sends)(functools.partial(lambda *at: copy(*at).wait_send(), part, direction))


def unpack_kernel(mixed, lesser_out, greater_out):
    for part, out in enumerate((lesser_out, greater_out)):
        held = mixed[part]
        rows = lax.broadcasted_iota(jnp.int32, held.shape, 0)
        lanes = lanes_of(held)
        mirrored = held.T
        out[0] = jnp.where(rows > lanes, held, jnp.where(rows < lanes, -mirrored, 0.0))
        out[1] = jnp.where(rows > lanes, mirrored, held)


def vmem(count):
    return [pl.BlockSpec(memory_space=pltpu.VMEM)] * count


def on_pair(hamiltonian, coupling, contact_rates, occupation, lesser_in, greater_in, phonon_shift):
    energy_count = lax.axis_size("energy")
    orbitals = hamiltonian.shape[1]
    half = coupling.shape[1]
    packed_pair = jax.ShapeDtypeStruct((2, orbitals, orbitals), jnp.float32)
    corners = pltpu.VMEM((2, half, orbitals), jnp.float32)
    payload = pl.pallas_call(
        pair_kernel,
        out_shape=packed_pair,
        in_specs=vmem(6),
        out_specs=vmem(1)[0],
        scratch_shapes=[corners, corners, pltpu.VMEM((half, half), jnp.float32)]
        + [pltpu.SemaphoreType.DMA((3,))] * 2,
        compiler_params=pltpu.CompilerParams(collective_id=0, has_side_effects=True),
    )(
        occupation[0],
        hamiltonian[0],
        coupling[0],
        contact_rates,
        lesser_in[0, 0, 0],
        greater_in[0, 0, 0],
    )

    def moved(steps, value):
        landing = pltpu.VMEM((2, orbitals, orbitals), jnp.float32)
        return pl.pallas_call(
            functools.partial(shift_kernel, steps),
            out_shape=packed_pair,
            in_specs=vmem(1),
            out_specs=vmem(1)[0],
            scratch_shapes=[landing, landing] + [pltpu.SemaphoreType.DMA((4,))] * 2,
            compiler_params=pltpu.CompilerParams(collective_id=steps, has_side_effects=True),
        )(value)

    limit = min(2**QUANTUM_BITS, energy_count // 2)
    mixed = lax.switch(
        phonon_shift[0] - 1,
        [functools.partial(moved, steps) for steps in range(1, max(limit, 2))],
        payload,
    )
    outs = pl.pallas_call(
        unpack_kernel,
        out_shape=(packed_pair, packed_pair),
        in_specs=vmem(1),
        out_specs=tuple(vmem(2)),
    )(mixed)
    return tuple(out[None, None, None] for out in outs)


def choose(hamiltonian, coupling, contact_rates, occupation, lesser_in, greater_in, phonon_shift):
    pair = lax.axis_size("dom") == 2 and hamiltonian.shape[0] == 1 and occupation.shape[0] == 1
    lanes_fit = hamiltonian.shape[1] == 2 * coupling.shape[1] and hamiltonian.shape[1] % 128 == 0
    program = on_pair if pair and lanes_fit else on_device
    return program(
        hamiltonian, coupling, contact_rates, occupation, lesser_in, greater_in, phonon_shift
    )


def solution(mesh):
    return jax.shard_map(
        choose,
        mesh=mesh,
        in_specs=(
            P("dom", None, None),
            P("dom", None, None),
            P(),
            P(None, "energy", None),
            P(None, "energy", "dom", None, None, None),
            P(None, "energy", "dom", None, None, None),
            P(),
        ),
        out_specs=(
            P(None, "energy", "dom", None, None, None),
            P(None, "energy", "dom", None, None, None),
        ),
        check_vma=False,
    )
```

```python
import functools

import jax
import jax.numpy as jnp
from jax import lax
from jax.experimental import pallas as pl
from jax.experimental.pallas import tpu as pltpu
from jax.sharding import PartitionSpec as P

QUANTUM_BITS = 6


highest = lax.Precision.HIGHEST
broadening = 0.2
phonon_bose = 0.4
phonon_strength = 0.5


def shifted(value, axis, steps):
    count = lax.axis_size(axis)
    leading, last = (max(0, -steps), min(count, count - steps))
    return lax.ppermute(value, axis, [(source, source + steps) for source in range(leading, last)])


def from_behind(value, axis, steps):
    count = lax.axis_size(axis)
    pairs = [(source, (source + steps) % count) for source in range(count)]
    return lax.ppermute(value, axis, pairs)


def matmul_high(first_factor, second_factor):
    return jnp.matmul(first_factor, second_factor, precision=highest)


def transposed(matrix):
    return jnp.swapaxes(matrix, -1, -2)


def complex_product(first_pair, second_pair):
    return (
        matmul_high(first_pair[0], second_pair[0]) - matmul_high(first_pair[1], second_pair[1]),
        matmul_high(first_pair[0], second_pair[1]) + matmul_high(first_pair[1], second_pair[0]),
    )


def adjoint(complex_pair):
    return (transposed(complex_pair[0]), -transposed(complex_pair[1]))


def inverted(complex_pair):
    real_part, imag_part = complex_pair
    orbitals = real_part.shape[-1]
    normal_real = matmul_high(transposed(real_part), real_part) + matmul_high(
        transposed(imag_part), imag_part
    )
    normal_imag = matmul_high(transposed(real_part), imag_part) - matmul_high(
        transposed(imag_part), real_part
    )
    stacked = jnp.concatenate(
        [
            jnp.concatenate([normal_real, -normal_imag], -1),
            jnp.concatenate([normal_imag, normal_real], -1),
        ],
        -2,
    )
    factor = jnp.linalg.cholesky(stacked)
    right_side = jnp.concatenate([transposed(real_part), -transposed(imag_part)], -2)
    middle = lax.linalg.triangular_solve(factor, right_side, left_side=True, lower=True)
    solved = lax.linalg.triangular_solve(
        factor, middle, left_side=True, lower=True, transpose_a=True
    )
    return (solved[..., :orbitals, :], solved[..., orbitals:, :])


def pad_first(corner, orbitals):
    extra = orbitals - corner.shape[-1]
    return jnp.pad(corner, ((0, 0), (0, extra), (0, extra)))


def pad_last(corner, orbitals):
    extra = orbitals - corner.shape[-1]
    return jnp.pad(corner, ((0, 0), (extra, 0), (extra, 0)))


def settle(runner, stored, inbound, outbound, active):
    return lax.cond(active, lambda: runner(inbound), lambda: (stored, outbound))


def pass_right(outbound):
    return shifted(outbound, "dom", 1)


def pass_left(outbound):
    return shifted(outbound, "dom", -1)


def on_device(
    hamiltonian, coupling, contact_rates, occupation, lesser_in, greater_in, phonon_shift
):
    dom_index = lax.axis_index("dom")
    dom_count = lax.axis_size("dom")
    energy_index = lax.axis_index("energy")
    energy_count = lax.axis_size("energy")
    local_energies = occupation.shape[0]
    local_blocks = hamiltonian.shape[0]
    orbitals = hamiltonian.shape[1]
    interface = coupling.shape[1]
    total_energies = local_energies * energy_count
    global_energy = jnp.arange(local_energies, dtype=jnp.int32) * energy_count + energy_index
    energy_value = -1.5 + 3.0 * global_energy.astype(jnp.float32) / (total_energies - 1)
    identity = jnp.eye(orbitals, dtype=jnp.float32)
    extra = orbitals - interface
    gamma_left = jnp.pad(jnp.diag(contact_rates[0]), ((0, extra), (0, extra)))
    last_coupling = coupling[local_blocks - 1]
    gamma_right = jnp.pad(
        matmul_high(last_coupling * contact_rates[1][None, :], transposed(last_coupling)),
        ((extra, 0), (extra, 0)),
    )
    at_left = (dom_index == 0).astype(jnp.float32)
    at_right = (dom_index == dom_count - 1).astype(jnp.float32)

    def system(position):
        onsite = 0.5 * (hamiltonian[position] + hamiltonian[position].T)
        lesser_block = lesser_in[:, 0, position]
        greater_block = greater_in[:, 0, position]
        matrix_real = (
            energy_value[:, None, None] * identity
            - onsite
            - 0.5 * (greater_block[:, 0] - lesser_block[:, 0])
        )
        matrix_imag = broadening * identity - 0.5 * (greater_block[:, 1] - lesser_block[:, 1])
        source_imag = lesser_block[:, 1]
        matrix_imag = matrix_imag + 0.5 * at_left * gamma_left
        source_imag = source_imag + at_left * occupation[:, 0, 0, None, None] * gamma_left
        matrix_imag = matrix_imag + 0.5 * at_right * gamma_right
        source_imag = source_imag + at_right * occupation[:, 0, 1, None, None] * gamma_right
        return ((matrix_real, matrix_imag), (lesser_block[:, 0], source_imag))

    def trailing(green_block, lesser_block):
        return jnp.stack(
            [
                green_block[0][..., -interface:, -interface:],
                green_block[1][..., -interface:, -interface:],
                lesser_block[0][..., -interface:, -interface:],
                lesser_block[1][..., -interface:, -interface:],
            ]
        )

    def leading(green_block, lesser_block):
        return jnp.stack(
            [
                green_block[0][..., :interface, :interface],
                green_block[1][..., :interface, :interface],
                lesser_block[0][..., :interface, :interface],
                lesser_block[1][..., :interface, :interface],
            ]
        )

    def left_sweep(inbound):
        boundary = inbound
        matrix, source = system(0)
        matrix = (
            matrix[0] - pad_first(boundary[0], orbitals),
            matrix[1] - pad_first(boundary[1], orbitals),
        )
        source = (
            source[0] + pad_first(boundary[2], orbitals),
            source[1] + pad_first(boundary[3], orbitals),
        )
        green_block = inverted(matrix)
        lesser_block = complex_product(complex_product(green_block, source), adjoint(green_block))
        kept_blocks = [boundary]
        link_block = coupling[0]
        boundary = matmul_high(
            transposed(link_block), matmul_high(trailing(green_block, lesser_block), link_block)
        )
        return (jnp.stack(kept_blocks, 2), boundary)

    def right_sweep(inbound):
        corner = inbound
        kept_blocks = [None] * local_blocks
        for position in reversed(range(local_blocks)):
            link_block = coupling[position]
            boundary = matmul_high(link_block, matmul_high(corner, transposed(link_block)))
            matrix, source = system(position)
            matrix = (
                matrix[0] - pad_last(boundary[0], orbitals),
                matrix[1] - pad_last(boundary[1], orbitals),
            )
            source = (
                source[0] + pad_last(boundary[2], orbitals),
                source[1] + pad_last(boundary[3], orbitals),
            )
            green_block = inverted(matrix)
            lesser_block = complex_product(
                complex_product(green_block, source), adjoint(green_block)
            )
            kept_blocks[position] = boundary
            corner = leading(green_block, lesser_block)
        return (jnp.stack(kept_blocks, 2), corner)

    def ascending(section_number):
        return section_number

    def descending(section_number):
        return dom_count - 1 - section_number

    zeros_out = jnp.zeros((4, local_energies, interface, interface), jnp.float32)
    zeros_bounds = jnp.zeros((4, local_energies, local_blocks, interface, interface), jnp.float32)

    def left_runner(inbound):
        return left_sweep(inbound)

    runners = [left_runner, right_sweep]
    orderings = [ascending, descending]
    senders = [pass_right, pass_left]
    stores = [zeros_bounds, zeros_bounds]
    outbounds = [zeros_out, zeros_out]

    def advance(section_number, stores, inbounds, outbounds):
        new_stores = []
        new_outbounds = []
        for chain_number in range(len(runners)):
            active = dom_index == orderings[chain_number](section_number)
            settled = settle(
                runners[chain_number],
                stores[chain_number],
                inbounds[chain_number],
                outbounds[chain_number],
                active,
            )
            new_stores.append(settled[0])
            new_outbounds.append(settled[1])
        return (new_stores, new_outbounds)

    def turn(section_number, loop_state):
        stores, inbounds, outbounds = loop_state
        stores, outbounds = advance(section_number, stores, inbounds, outbounds)
        inbounds = [
            senders[chain_number](outbounds[chain_number]) for chain_number in range(len(runners))
        ]
        return (stores, inbounds, outbounds)

    inbounds = [jnp.zeros_like(outbound) for outbound in outbounds]
    stores, inbounds, outbounds = lax.fori_loop(
        0, dom_count - 1, turn, (stores, inbounds, outbounds)
    )
    stores, outbounds = advance(dom_count - 1, stores, inbounds, outbounds)
    left_store, right_store = stores
    position = 0
    left_part = left_store[:, :, position]
    right_part = right_store[:, :, position]
    matrix, source = system(position)
    matrix = (
        matrix[0] - pad_first(left_part[0], orbitals) - pad_last(right_part[0], orbitals),
        matrix[1] - pad_first(left_part[1], orbitals) - pad_last(right_part[1], orbitals),
    )
    source = (
        source[0] + pad_first(left_part[2], orbitals) + pad_last(right_part[2], orbitals),
        source[1] + pad_first(left_part[3], orbitals) + pad_last(right_part[3], orbitals),
    )
    green_block = inverted(matrix)
    lesser_block = complex_product(complex_product(green_block, source), adjoint(green_block))
    kept_final = [jnp.stack([green_block[0], green_block[1], lesser_block[0], lesser_block[1]])]
    final_store = jnp.stack(kept_final, 2)
    green_real = final_store[0]
    green_imag = final_store[1]
    lesser_real = final_store[2]
    lesser_imag = final_store[3]
    greater_real = lesser_real + green_real - transposed(green_real)
    greater_imag = lesser_imag + green_imag + transposed(green_imag)
    shift_amount = phonon_shift[0]
    quantum_limit = min(2**QUANTUM_BITS, total_energies // 2)
    bit_count = (quantum_limit - 1).bit_length()

    def moved_by(payload, direction):
        for bit_number in range(bit_count):
            amount = direction * 2**bit_number
            remainder = amount % energy_count
            carried = amount // energy_count
            arrived = from_behind(payload, "energy", remainder)
            aligned = jnp.where(
                energy_index < remainder,
                jnp.roll(arrived, carried + 1, axis=1),
                jnp.roll(arrived, carried, axis=1),
            )
            chosen = jnp.right_shift(shift_amount, bit_number) & 1 == 1
            payload = jnp.where(chosen, aligned, payload)
        return payload

    payload = jnp.stack([lesser_real, lesser_imag, greater_real, greater_imag])
    below = moved_by(payload, 1)
    above = moved_by(payload, -1)
    below_lesser = (below[0], below[1])
    below_greater = (below[2], below[3])
    above_lesser = (above[0], above[1])
    above_greater = (above[2], above[3])
    below_source = global_energy - shift_amount
    above_source = global_energy + shift_amount
    valid_below = ((below_source >= 0) & (below_source < total_energies)).astype(jnp.float32)[
        :, None, None, None
    ]
    valid_above = ((above_source >= 0) & (above_source < total_energies)).astype(jnp.float32)[
        :, None, None, None
    ]
    lesser_out_real = phonon_strength * (
        (phonon_bose + 1.0) * (above_lesser[0] * valid_above)
        + phonon_bose * (below_lesser[0] * valid_below)
    )
    lesser_out_imag = phonon_strength * (
        (phonon_bose + 1.0) * (above_lesser[1] * valid_above)
        + phonon_bose * (below_lesser[1] * valid_below)
    )
    greater_out_real = phonon_strength * (
        (phonon_bose + 1.0) * (below_greater[0] * valid_below)
        + phonon_bose * (above_greater[0] * valid_above)
    )
    greater_out_imag = phonon_strength * (
        (phonon_bose + 1.0) * (below_greater[1] * valid_below)
        + phonon_bose * (above_greater[1] * valid_above)
    )
    lesser_out = jnp.stack([lesser_out_real, lesser_out_imag], 2)[:, None]
    greater_out = jnp.stack([greater_out_real, greater_out_imag], 2)[:, None]
    return (lesser_out, greater_out)


MESH = pl.DeviceIdType.MESH
ROWS_BY_ROWS = (((1,), (1,)), ((), ()))
ROWS_BY_COLUMNS = (((1,), (0,)), ((), ()))


def dot(first, second, dims=ROWS_BY_COLUMNS):
    return lax.dot_general(
        first, second, dims, precision=highest, preferred_element_type=jnp.float32
    )


def lanes_of(array):
    return lax.broadcasted_iota(jnp.int32, array.shape, 1)


def times_i(wide):
    half = wide.shape[1] // 2
    moved = pltpu.roll(wide, half, 1)
    return jnp.where(lanes_of(wide) < half, -moved, moved)


def embedded(wide):
    return jnp.concatenate([wide, times_i(wide)], 0)


def wide_product(first, second):
    return dot(first, embedded(second))


def wide_product_adjoint(first, second):
    return dot(first, embedded(second), ROWS_BY_ROWS)


def twice_diagonal(matrix):
    zero = jnp.zeros_like(matrix)
    return jnp.concatenate(
        [jnp.concatenate([matrix, zero], 1), jnp.concatenate([zero, matrix], 1)], 0
    )


def sandwiched(matrix, wide):
    return dot(dot(matrix, wide), twice_diagonal(matrix), ROWS_BY_ROWS)


def scaled_row(real, imag, row):
    plain, turned = row
    return (real * plain + imag * turned, real * turned - imag * plain)


def wide_inverse(wide, group=4):
    size = wide.shape[0]
    rows = lax.broadcasted_iota(jnp.int32, wide.shape, 0)
    lanes = lanes_of(wide)
    row_lanes = lax.broadcasted_iota(jnp.int32, (1, wide.shape[1]), 1)
    for start in range(0, size, group):
        members = range(group)
        in_lanes = (lanes >= start) & (lanes < start + group)
        in_lanes = in_lanes | ((lanes >= size + start) & (lanes < size + start + group))
        in_rows = (rows >= start) & (rows < start + group)
        picked = (row_lanes >= start) & (row_lanes < start + group)
        picked = picked | ((row_lanes >= size + start) & (row_lanes < size + start + group))
        corner, held = [], []
        for member in members:
            row = wide[start + member : start + member + 1, :]
            corner.append(
                [
                    tuple(
                        jnp.broadcast_to(row[:, lane : lane + 1], row.shape)
                        for lane in (start + other, size + start + other)
                    )
                    for other in members
                ]
            )
            turned = jnp.where(picked, 0.0, times_i(row))
            row = jnp.where(picked, 0.0, row)
            row = jnp.where(row_lanes == start + member, 1.0, row)
            turned = jnp.where(row_lanes == size + start + member, 1.0, turned)
            held.append((row, turned))
        for pivot in members:
            real, imag = corner[pivot][pivot]
            scale = 1.0 / (real * real + imag * imag)
            real, imag = real * scale, -imag * scale
            held[pivot] = scaled_row(real, imag, held[pivot])
            for other in range(pivot + 1, group):
                entry = corner[pivot][other]
                corner[pivot][other] = (
                    real * entry[0] - imag * entry[1],
                    real * entry[1] + imag * entry[0],
                )
            for member in members:
                if member == pivot:
                    continue
                real, imag = corner[member][pivot]
                for other in range(pivot + 1, group):
                    entry, kept = corner[pivot][other], corner[member][other]
                    corner[member][other] = (
                        kept[0] - (real * entry[0] - imag * entry[1]),
                        kept[1] - (real * entry[1] + imag * entry[0]),
                    )
                lost = scaled_row(real, imag, held[pivot])
                held[member] = (held[member][0] - lost[0], held[member][1] - lost[1])
        updated = jnp.where(in_rows | in_lanes, 0.0, wide)
        for member in members:
            lane = start + member
            column_real = jnp.broadcast_to(wide[:, lane : lane + 1], wide.shape)
            lane = size + lane
            column_imag = jnp.broadcast_to(wide[:, lane : lane + 1], wide.shape)
            at_member = (rows == start + member).astype(jnp.float32)
            column_real = jnp.where(in_rows, -at_member, column_real)
            column_imag = jnp.where(in_rows, 0.0, column_imag)
            updated = updated - column_real * held[member][0] - column_imag * held[member][1]
        wide = updated
    return wide


def flipped(flag, matrix):
    half = matrix.shape[0] // 2
    moved = pltpu.roll(matrix, half, 1)
    moved = jnp.concatenate([moved[half:], moved[:half]], 0)
    return jnp.where(flag, moved, matrix)


def wide_quarters(real, imag):
    half = real.shape[0] // 2
    left_lanes = lax.broadcasted_iota(jnp.int32, (half, 2 * half), 1) < half
    quarters = []
    for start in (0, half):
        real_rows, imag_rows = real[start : start + half], imag[start : start + half]
        quarters.append(jnp.where(left_lanes, real_rows, pltpu.roll(imag_rows, half, 1)))
        quarters.append(jnp.where(left_lanes, pltpu.roll(real_rows, half, 1), imag_rows))
    return quarters


def real_imag_rows(left, right):
    half = left.shape[0]
    left_lanes = lanes_of(left) < half
    return (
        jnp.where(left_lanes, left, pltpu.roll(right, half, 1)),
        jnp.where(left_lanes, pltpu.roll(left, half, 1), right),
    )


def unit(size):
    rows = lax.broadcasted_iota(jnp.int32, (size, size), 0)
    return (rows == lax.broadcasted_iota(jnp.int32, (size, size), 1)).astype(jnp.float32)


def packed(real, imag):
    rows = lax.broadcasted_iota(jnp.int32, real.shape, 0)
    return jnp.where(rows > lanes_of(real), real, imag)


def pair_kernel(
    occupation,
    hamiltonian,
    coupling,
    rates,
    lesser,
    greater,
    payload,
    outgoing_corners,
    arrived,
    arrived_link,
    send_sems,
    recv_sems,
):
    place = lax.axis_index("dom")
    partner = 1 - place
    barrier = pltpu.get_barrier_semaphore()
    pl.semaphore_signal(barrier, inc=1, device_id={"dom": partner}, device_id_type=MESH)
    flag = place == 1
    energy_index = lax.axis_index("energy").astype(jnp.float32)
    energy_value = -1.5 + 3.0 * energy_index / (lax.axis_size("energy") - 1)
    orbitals = hamiltonian.shape[0]
    half = coupling.shape[0]
    identity = unit(orbitals)
    link = coupling[...]
    system_real = (
        energy_value * identity
        - 0.5 * (hamiltonian[...] + hamiltonian[...].T)
        - 0.5 * (greater[0] - lesser[0])
    )
    system_imag = broadening * identity - 0.5 * (greater[1] - lesser[1])
    system_real = flipped(flag, system_real)
    system_imag = flipped(flag, system_imag)
    source_real = flipped(flag, lesser[0])
    source_imag = flipped(flag, lesser[1])
    small = unit(half)
    left_gamma = small * rates[0:1, :]
    right_gamma = dot(link * rates[1:2, :], link, ROWS_BY_ROWS)
    gamma = jnp.where(flag, right_gamma, left_gamma)
    zero = jnp.zeros_like(gamma)
    gamma_turned = jnp.concatenate([zero, gamma], 1)
    inner, upper, lower, outer = wide_quarters(system_real, system_imag)
    inner = inner + 0.5 * gamma_turned
    filling = jnp.where(flag, occupation[:, 1:2], occupation[:, 0:1])
    gamma_padded = jnp.concatenate([gamma, zero], 1)
    source_imag = source_imag + filling * jnp.concatenate(
        [gamma_padded, jnp.zeros_like(gamma_padded)], 0
    )
    inverse = wide_inverse(inner)
    copies = [
        pltpu.make_async_remote_copy(
            src_ref=origin,
            dst_ref=target,
            send_sem=send_sems.at[part],
            recv_sem=recv_sems.at[part],
            device_id={"dom": partner},
            device_id_type=MESH,
        )
        for part, (origin, target) in enumerate(
            (
                (outgoing_corners.at[0], arrived.at[0]),
                (outgoing_corners.at[1], arrived.at[1]),
                (coupling, arrived_link),
            )
        )
    ]
    pl.semaphore_wait(barrier, 1)
    copies[2].start()
    right = wide_product(inverse, upper)
    left = wide_product(lower, inverse)
    schur = outer - wide_product(left, upper)
    corner = wide_inverse(schur)
    outgoing_corners[0] = corner
    copies[0].start()
    first, above, below, last = wide_quarters(source_real, source_imag)
    reduced = last - wide_product(left, above) - wide_product_adjoint(below, left)
    reduced = reduced + wide_product_adjoint(wide_product(left, first), left)
    corner_lesser = wide_product_adjoint(wide_product(corner, reduced), corner)
    outgoing_corners[1] = corner_lesser
    copies[1].start()
    copies[2].wait()
    incoming = jnp.where(flag, arrived_link[...].T, link)
    copies[0].wait()
    last = wide_inverse(schur - sandwiched(incoming, arrived[0]))
    copies[1].wait()
    boundary_lesser = sandwiched(incoming, arrived[1])
    lower = wide_product(last, left)
    upper = -wide_product(right, last)
    inner = inverse + wide_product(right, lower)
    top_real, top_imag = real_imag_rows(inner, upper)
    bottom_real, bottom_imag = real_imag_rows(-lower, last)
    green_real = jnp.concatenate([top_real, bottom_real], 0)
    green_imag = jnp.concatenate([top_imag, bottom_imag], 0)
    green = jnp.concatenate([green_real, green_imag], 1)
    added_real, added_imag = real_imag_rows(jnp.zeros_like(boundary_lesser), boundary_lesser)
    source = jnp.concatenate([source_real, source_imag], 1)
    source_bottom = source[half:, :] + jnp.concatenate([added_real, added_imag], 1)
    sources = jnp.concatenate([source[:half, :], source_bottom], 0)
    lesser = wide_product_adjoint(wide_product(green, sources), green)
    lesser_real = flipped(flag, lesser[:, :orbitals])
    lesser_imag = flipped(flag, lesser[:, orbitals:])
    spectral_real = flipped(flag, green_real - green_real.T)
    spectral_imag = flipped(flag, green_imag + green_imag.T)
    payload[0] = packed(lesser_real, lesser_imag)
    payload[1] = packed(lesser_real + spectral_real, lesser_imag + spectral_imag)


def shift_kernel(steps, payload, mixed, below, above, send_sems, recv_sems):
    here = lax.axis_index("energy")
    count = lax.axis_size("energy")
    has_below, has_above = here >= steps, here + steps < count
    lower, higher = jnp.maximum(here - steps, 0), jnp.minimum(here + steps, count - 1)
    barrier = pltpu.get_barrier_semaphore()

    def copy(part, direction):
        slot = 2 * part + direction
        return pltpu.make_async_remote_copy(
            src_ref=payload.at[part],
            dst_ref=(below, above)[direction].at[part],
            send_sem=send_sems.at[slot],
            recv_sem=recv_sems.at[slot],
            device_id={"energy": (higher, lower)[direction]},
            device_id_type=MESH,
        )

    @pl.when(has_below)
    def _():
        pl.semaphore_signal(barrier, inc=1, device_id={"energy": lower}, device_id_type=MESH)

    @pl.when(has_above)
    def _():
        pl.semaphore_signal(barrier, inc=1, device_id={"energy": higher}, device_id_type=MESH)

    @pl.when(jnp.logical_not(has_below))
    def _():
        below[...] = jnp.zeros_like(below)

    @pl.when(jnp.logical_not(has_above))
    def _():
        above[...] = jnp.zeros_like(above)

    pl.semaphore_wait(barrier, has_below.astype(jnp.int32) + has_above.astype(jnp.int32))

    for part in range(2):
        for direction, sends in ((0, has_above), (1, has_below)):
            pl.when(sends)(functools.partial(lambda *at: copy(*at).start(), part, direction))
    emitted = phonon_strength * (phonon_bose + 1.0)
    absorbed = phonon_strength * phonon_bose
    for part, (from_below, from_above) in enumerate(((absorbed, emitted), (emitted, absorbed))):
        for direction, receives in ((0, has_below), (1, has_above)):
            pl.when(receives)(functools.partial(lambda *at: copy(*at).wait_recv(), part, direction))
        mixed[part] = from_below * below[part] + from_above * above[part]
    for part in range(2):
        for direction, sends in ((0, has_above), (1, has_below)):
            pl.when(sends)(functools.partial(lambda *at: copy(*at).wait_send(), part, direction))


def unpack_kernel(mixed, lesser_out, greater_out):
    for part, out in enumerate((lesser_out, greater_out)):
        held = mixed[part]
        rows = lax.broadcasted_iota(jnp.int32, held.shape, 0)
        lanes = lanes_of(held)
        mirrored = held.T
        out[0] = jnp.where(rows > lanes, held, jnp.where(rows < lanes, -mirrored, 0.0))
        out[1] = jnp.where(rows > lanes, mirrored, held)


def vmem(count):
    return [pl.BlockSpec(memory_space=pltpu.VMEM)] * count


def on_pair(hamiltonian, coupling, contact_rates, occupation, lesser_in, greater_in, phonon_shift):
    energy_count = lax.axis_size("energy")
    orbitals = hamiltonian.shape[1]
    half = coupling.shape[1]
    packed_pair = jax.ShapeDtypeStruct((2, orbitals, orbitals), jnp.float32)
    corners = pltpu.VMEM((2, half, orbitals), jnp.float32)
    payload = pl.pallas_call(
        pair_kernel,
        out_shape=packed_pair,
        in_specs=vmem(6),
        out_specs=vmem(1)[0],
        scratch_shapes=[corners, corners, pltpu.VMEM((half, half), jnp.float32)]
        + [pltpu.SemaphoreType.DMA((3,))] * 2,
        compiler_params=pltpu.CompilerParams(collective_id=0, has_side_effects=True),
    )(
        occupation[0],
        hamiltonian[0],
        coupling[0],
        contact_rates,
        lesser_in[0, 0, 0],
        greater_in[0, 0, 0],
    )

    def moved(steps, value):
        landing = pltpu.VMEM((2, orbitals, orbitals), jnp.float32)
        return pl.pallas_call(
            functools.partial(shift_kernel, steps),
            out_shape=packed_pair,
            in_specs=vmem(1),
            out_specs=vmem(1)[0],
            scratch_shapes=[landing, landing] + [pltpu.SemaphoreType.DMA((4,))] * 2,
            compiler_params=pltpu.CompilerParams(collective_id=steps, has_side_effects=True),
        )(value)

    limit = min(2**QUANTUM_BITS, energy_count // 2)
    mixed = lax.switch(
        phonon_shift[0] - 1,
        [functools.partial(moved, steps) for steps in range(1, max(limit, 2))],
        payload,
    )
    outs = pl.pallas_call(
        unpack_kernel,
        out_shape=(packed_pair, packed_pair),
        in_specs=vmem(1),
        out_specs=tuple(vmem(2)),
    )(mixed)
    return tuple(out[None, None, None] for out in outs)


def choose(hamiltonian, coupling, contact_rates, occupation, lesser_in, greater_in, phonon_shift):
    pair = lax.axis_size("dom") == 2 and hamiltonian.shape[0] == 1 and occupation.shape[0] == 1
    lanes_fit = hamiltonian.shape[1] == 2 * coupling.shape[1] and hamiltonian.shape[1] % 128 == 0
    program = on_pair if pair and lanes_fit else on_device
    return program(
        hamiltonian, coupling, contact_rates, occupation, lesser_in, greater_in, phonon_shift
    )


def solution(mesh):
    return jax.shard_map(
        choose,
        mesh=mesh,
        in_specs=(
            P("dom", None, None),
            P("dom", None, None),
            P(),
            P(None, "energy", None),
            P(None, "energy", "dom", None, None, None),
            P(None, "energy", "dom", None, None, None),
            P(),
        ),
        out_specs=(
            P(None, "energy", "dom", None, None, None),
            P(None, "energy", "dom", None, None, None),
        ),
        check_vma=False,
    )
```
